256 devices in a mesh: rows: 32 (over x, y, core), cols: 8 (over z).
Axes of the slice: x: 4, y: 4, z: 8, core: 2. Of those that a mesh axis runs over, the one named last changes fastest.
Arguments:
- basis: float32 [512, 32768], P(None, ('cols', 'rows')), may hold values from -6 to 6
- tile_counts: int32 [8192, 128, 128], P(('rows', 'cols')), may hold values from 0 to 63
- tile_rows: int32 [8192], P(('rows', 'cols')), may hold values from 0 to 7
- tile_cols: int32 [8192], P(('rows', 'cols')), may hold values from 0 to 31
- tile_live: int32 [256], P(('rows', 'cols')), may hold values from 8 to 32, as said below
- marginals: int32 [32768], replicated, may hold values from 1 to 983040, as said below
Outputs:
- subspace: float32 [512, 32768], P(None, ('cols', 'rows'))
The draws below stay inside these ranges and needn't reach their ends.
Inputs may be any that keep to these rules, and one draw needn't show every extreme that they name: `tile_live`: every list has at least a quarter of its 32 slots live; some list has all 32 live. `marginals`: A small multiplier times a power of four.
All inputs are finite; a program needn't handle non-finite values.
Results may differ from the reference program's by a relative error of at most 0.012.
The reference program's roundings to bfloat16 on the way (of `ppmi` and `rounded`) count: a program that leaves them out, or rounds other values in their place, can miss the bound.
Values may be sent and summed in bfloat16 or wider, within the bound.
No kernel may reach another device: no remote copies, remote signals or barrier semaphores. Data moves between devices by JAX's collectives and lax.ppermute only.
A program may use at most 128 MiB of HBM per device.

```python
import jax
import jax.numpy as jnp
from jax import lax

K = 512
BT = 128
TB_DEV = 128
TILES_DEV = 32
ITERS = 2
VOCAB = 32768
ROWBLK = 8
COLBLK = 32
N_ROWS = 32
N_COLS = 8


def draw_tile_live(key, part):
    key = jax.random.fold_in(key, 11)
    first_key, second_key = jax.random.split(key)
    counted = jax.random.randint(first_key, (N_ROWS * N_COLS,), TILES_DEV // 4, TILES_DEV + 1, dtype=jnp.int32)
    fullest = jax.random.randint(second_key, (), 0, N_ROWS * N_COLS, dtype=jnp.int32)
    return counted.at[fullest].set(TILES_DEV)


def draw_marginals(key, part):
    key = jax.random.fold_in(key, 23)
    first_key, second_key = jax.random.split(key)
    leading = jax.random.randint(first_key, (VOCAB,), 1, 16, dtype=jnp.int32)
    exponents = jax.random.randint(second_key, (VOCAB,), 0, 9, dtype=jnp.int32)
    return leading * jnp.left_shift(jnp.ones_like(exponents), 2 * exponents)


def with_ends(array, own_key, low, top_value):
    place = [jax.random.randint(jax.random.fold_in(own_key, axis), (), 0, length) for axis, length in enumerate(array.shape)]
    main_axis = array.shape.index(max(array.shape))
    neighbour = place[:main_axis] + [(place[main_axis] + 1) % array.shape[main_axis]] + place[main_axis + 1:]
    return array.at[tuple(place)].set(low).at[tuple(neighbour)].set(top_value)


def block_levels(stream_key, extent, shards, low, top_value):
    factor_of = 1.0
    for dim, blocks in shards:
        heights = jax.random.uniform(jax.random.fold_in(jax.random.fold_in(stream_key, 6), dim), (blocks,), jnp.float32, low / len(shards), top_value / len(shards))
        factor_of = factor_of * jnp.repeat(jnp.exp(heights), extent[dim] // blocks).reshape((-1,) + (1,) * (len(extent) - 1 - dim))
    return factor_of


def scatter_about(key, extent, width, limit, pieces=(), kind=jnp.bfloat16):
    result = width * jax.random.normal(key, extent, jnp.float32)
    if pieces:
        result = result * block_levels(key, extent, pieces, -0.22, 0.18)
    return jnp.clip(result, -limit, limit).astype(kind)


def setup_inputs(seed: int = 0) -> dict:
    key_list = jax.random.split(jax.random.key(seed), 7)
    basis = scatter_about(key_list[0], (K, VOCAB), 1.0, 6.0, ((1, 256),), jnp.float32)
    tile_counts = with_ends(jax.random.randint(key_list[1], (N_ROWS * N_COLS * TILES_DEV, BT, BT), 0, 64), jax.random.fold_in(key_list[1], 1), 0, 63).astype(jnp.int32)
    tile_rows = with_ends(jax.random.randint(key_list[2], (N_ROWS * N_COLS * TILES_DEV,), 0, ROWBLK), jax.random.fold_in(key_list[2], 1), 0, ROWBLK - 1).astype(jnp.int32)
    tile_cols = with_ends(jax.random.randint(key_list[3], (N_ROWS * N_COLS * TILES_DEV,), 0, COLBLK), jax.random.fold_in(key_list[3], 1), 0, COLBLK - 1).astype(jnp.int32)
    tile_live = draw_tile_live(jax.random.fold_in(key_list[6], 71), 0)
    marginals = draw_marginals(jax.random.fold_in(key_list[6], 71), 0)
    return dict(basis=basis, tile_counts=tile_counts, tile_rows=tile_rows, tile_cols=tile_cols, tile_live=tile_live, marginals=marginals)


def reference(basis, tile_counts, tile_rows, tile_cols, tile_live, marginals):
    devices_all = N_ROWS * N_COLS
    group_size = N_ROWS * TB_DEV
    row_blocks = N_COLS * TB_DEV // BT
    marg_float = marginals.astype(jnp.float32)
    grand_total = jnp.sum(marg_float)
    log_margins = jnp.log(marg_float)
    stacked_logs = log_margins.reshape(N_COLS, N_ROWS, TB_DEV)
    counts_all = tile_counts.reshape(devices_all, TILES_DEV, BT, BT)
    rows_all = tile_rows.reshape(devices_all, TILES_DEV)
    cols_all = tile_cols.reshape(devices_all, TILES_DEV)
    position = jnp.arange(TILES_DEV, dtype=jnp.int32)
    block_ids = jnp.arange(row_blocks, dtype=jnp.int32)
    current = basis
    for sweep_index in range(ITERS):
        rounded = lax.optimization_barrier(current.astype(jnp.bfloat16))

        def one_device(running, device):
            row_index = device // N_COLS
            col_index = device % N_COLS
            row_logs = lax.dynamic_index_in_dim(stacked_logs, row_index, 1, keepdims=False).reshape(-1, BT)
            col_logs = lax.dynamic_slice_in_dim(log_margins, col_index * group_size, group_size).reshape(-1, BT)
            counts_here = lax.dynamic_index_in_dim(counts_all, device, 0, keepdims=False)
            rows_here = lax.dynamic_index_in_dim(rows_all, device, 0, keepdims=False)
            cols_here = lax.dynamic_index_in_dim(cols_all, device, 0, keepdims=False)
            live_here = lax.dynamic_index_in_dim(tile_live, device, 0, keepdims=False)
            counts_float = counts_here.astype(jnp.float32)
            log_ratio = jnp.log(jnp.maximum(counts_float, 1.0)) + jnp.log(grand_total) - jnp.take(row_logs, rows_here, axis=0)[:, :, None] - jnp.take(col_logs, cols_here, axis=0)[:, None, :]
            keep_mask = (counts_here > 0) & (position < live_here)[:, None, None]
            ppmi = lax.optimization_barrier(jnp.where(keep_mask, jnp.maximum(log_ratio, 0.0), 0.0).astype(jnp.bfloat16))
            group_basis = lax.dynamic_slice_in_dim(rounded, col_index * group_size, group_size, 1).reshape(K, -1, BT)
            picked = jnp.take(group_basis, cols_here, axis=1)
            products = jnp.einsum('ktc,trc->ktr', picked.astype(jnp.float32), ppmi.astype(jnp.float32))
            onehot = (rows_here[:, None] == block_ids[None, :]).astype(jnp.float32)
            placed = jnp.einsum('ktr,ta->kar', products, onehot, precision=lax.Precision.HIGHEST)
            placed = placed.reshape(K, N_COLS, TB_DEV)
            previous = lax.dynamic_index_in_dim(running, row_index, 2, keepdims=False)
            running = lax.dynamic_update_index_in_dim(running, previous + placed, row_index, 2)
            return (running, None)
        zero_sum = jnp.zeros((K, N_COLS, N_ROWS, TB_DEV), jnp.float32)
        summed, unused = lax.scan(one_device, zero_sum, jnp.arange(devices_all, dtype=jnp.int32))
        full_image = summed.reshape(K, N_COLS * N_ROWS * TB_DEV)
        gram_matrix = jnp.dot(full_image.astype(jnp.float32), full_image.T.astype(jnp.float32), precision=lax.Precision.HIGHEST, preferred_element_type=jnp.float32)
        factor = jnp.linalg.cholesky(gram_matrix)
        current = jax.scipy.linalg.solve_triangular(factor, full_image, lower=True)
    return current
```

```python
import jax
import jax.numpy as jnp
from jax import lax
from jax.experimental import pallas as pl
from jax.experimental.pallas import tpu as pltpu
from jax.sharding import Mesh, PartitionSpec as P

ITERS = 2
HIGHEST = lax.Precision.HIGHEST
TILE = 128
SUB = 8
BLOCKS = 4
PAIRS = [(i, j) for i in range(BLOCKS) for j in range(i + 1)]
PLACE = {pair: n for n, pair in enumerate(PAIRS)}
HALF = len(PAIRS) // 2
VMEM_LIMIT = 56 * 1024 * 1024
ROWS = ("x", "y", "core")
PLANE = ("x", "y")
VMEM = pl.BlockSpec(memory_space=pltpu.VMEM)
SMEM = pl.BlockSpec(memory_space=pltpu.SMEM)


def dot_nt(a, b, precision=HIGHEST):
    return lax.dot_general(
        a, b, (((1,), (1,)), ((), ())), precision=precision, preferred_element_type=jnp.float32
    )


def dot_nn(a, b):
    return jnp.dot(a, b, precision=HIGHEST, preferred_element_type=jnp.float32)


def call(kernel, out_shape, in_specs, scratch=()):
    return pl.pallas_call(
        kernel,
        out_shape=out_shape,
        in_specs=in_specs,
        out_specs=VMEM,
        scratch_shapes=list(scratch),
        compiler_params=pltpu.CompilerParams(vmem_limit_bytes=VMEM_LIMIT),
    )


def multiply_kernel(live_ref, rows_ref, cols_ref, basis_ref, ppmi_ref, out_ref):
    out_ref[...] = jnp.zeros_like(out_ref)

    def add_tile(t, carry):
        r = rows_ref[t]
        product = dot_nt(basis_ref[cols_ref[t]], ppmi_ref[t], None)
        out_ref[r] = out_ref[r] + product
        return carry

    lax.fori_loop(0, live_ref[0], add_tile, 0)


def gram_kernel(core_ref, own_ref, other_ref, out_ref):
    for n in range(HALF):
        first, second = PAIRS[n], PAIRS[HALF + n]
        core = core_ref[0]
        i = pl.multiple_of(jnp.where(core == 0, first[0], second[0]) * TILE, TILE)
        j = pl.multiple_of(jnp.where(core == 0, first[1], second[1]) * TILE, TILE)
        out_ref[n] = dot_nt(own_ref[pl.ds(i, TILE), :], own_ref[pl.ds(j, TILE), :]) + dot_nt(
            other_ref[pl.ds(i, TILE), :], other_ref[pl.ds(j, TILE), :]
        )


def spread_row(x, m):
    return jnp.broadcast_to(x[m : m + 1, :], (SUB, TILE))


def spread_col(x, lane):
    return jnp.broadcast_to(x[:, lane : lane + 1], (SUB, TILE))


def factor_inverse(read, write):
    n = TILE // SUB
    a = [read(i) for i in range(n)]
    row = lax.broadcasted_iota(jnp.int32, (SUB, TILE), 0)
    lane = lax.broadcasted_iota(jnp.int32, (SUB, TILE), 1)
    m = [jnp.where(lane == row + SUB * i, 1.0, 0.0).astype(jnp.float32) for i in range(n)]
    for p in range(n):
        cols = [[spread_col(a[i], SUB * p + k) for i in range(p, n)] for k in range(SUB)]
        s = [[spread_row(cols[k][0], q) if q >= k else None for k in range(SUB)] for q in range(SUB)]
        u = [spread_row(a[p], k) for k in range(SUB)]
        v = [spread_row(m[p], k) for k in range(SUB)]
        following = [cols[k][1] for k in range(SUB)] if p + 1 < n else None
        low = [[None] * SUB for _ in range(SUB)]
        root = [None] * SUB
        for k in range(SUB):
            root[k] = lax.rsqrt(s[k][k])
            for q in range(k + 1, SUB):
                low[q][k] = s[q][k] * root[k]
            for q in range(k + 1, SUB):
                for t in range(k + 1, q + 1):
                    s[q][t] = s[q][t] - low[q][k] * low[t][k]
            u[k] = u[k] * root[k]
            v[k] = v[k] * root[k]
            for q in range(k + 1, SUB):
                u[q] = u[q] - low[q][k] * u[k]
                v[q] = v[q] - low[q][k] * v[k]
            if following is not None:
                following[k] = following[k] * root[k]
                for q in range(k + 1, SUB):
                    following[q] = following[q] - low[q][k] * following[k]
        for k in range(SUB):
            write(SUB * p + k, v[k])
        if p + 1 == n:
            break
        for k in range(SUB):
            a[p + 1] = a[p + 1] - following[k] * u[k]
        zu = [None] * SUB
        zv = [None] * SUB
        for k in reversed(range(SUB)):
            x, y = u[k], v[k]
            for q in range(k + 1, SUB):
                x = x - low[q][k] * zu[q]
                y = y - low[q][k] * zv[q]
            zu[k] = x * root[k]
            zv[k] = y * root[k]
        for i in range(p + 1, n):
            for k in range(SUB):
                if i > p + 1:
                    a[i] = a[i] - cols[k][i - p] * zu[k]
                m[i] = m[i] - cols[k][i - p] * zv[k]


def solve_kernel(core_ref, own_ref, other_ref, image_ref, out_ref, a_ref, w_ref):
    core = core_ref[0]
    for n in range(HALF):
        a_ref[core * HALF + n] = own_ref[n]
        a_ref[(1 - core) * HALF + n] = other_ref[n]
    factor = {}
    solved = []
    for j in range(BLOCKS):
        here = PLACE[j, j]

        def read(i):
            return a_ref[here, pl.ds(SUB * i, SUB), :]

        def write(r, value):
            w_ref[pl.ds(r, 1), :] = value[0:1, :]

        factor_inverse(read, write)
        inverse = w_ref[...]
        for i in range(j + 1, BLOCKS):
            factor[i, j] = dot_nt(a_ref[PLACE[i, j]], inverse)
        for i in range(j + 1, BLOCKS):
            for k in range(j + 1, i + 1):
                n = PLACE[i, k]
                a_ref[n] = a_ref[n] - dot_nt(factor[i, j], factor[k, j])
        rest = image_ref[pl.ds(TILE * j, TILE), :]
        for i in range(j):
            rest = rest - dot_nn(factor[j, i], solved[i])
        solved.append(dot_nn(inverse, rest))
        out_ref[pl.ds(TILE * j, TILE), :] = solved[j]


def swap_core(x):
    return lax.ppermute(x, "core", [(0, 1), (1, 0)])


def gram_sum(core, image):
    k, width = image.shape
    plane = lax.axis_size(PLANE)
    depth = lax.axis_size("z")
    part = call(
        gram_kernel, jax.ShapeDtypeStruct((HALF, TILE, TILE), jnp.float32), [SMEM, VMEM, VMEM]
    )(core, image, swap_core(image))
    part = part.reshape(plane, HALF * TILE // plane, TILE)
    part = jnp.sum(lax.all_to_all(part, PLANE, 0, 0), axis=0)
    part = jnp.broadcast_to(part[None], (depth,) + part.shape)
    part = jnp.sum(lax.all_to_all(part, "z", 0, 0), axis=0)
    part = jnp.broadcast_to(part[None], (plane,) + part.shape)
    part = lax.all_to_all(part, PLANE, 0, 0)
    part = part.reshape(HALF, TILE, TILE)
    return part, swap_core(part)


def local(basis, tile_counts, tile_rows, tile_cols, tile_live, marginals):
    width_k, terms_here = basis.shape
    capacity, tile_size, _ = tile_counts.shape
    row_count = lax.axis_size(ROWS)
    col_count = lax.axis_size("z")
    row_index = lax.axis_index(ROWS)
    col_index = lax.axis_index("z")
    core = lax.axis_index("core").astype(jnp.int32).reshape(1)
    group_size = row_count * terms_here
    gathered = lax.all_gather(basis.astype(jnp.bfloat16), ROWS, axis=0)
    marg_float = marginals.astype(jnp.float32)
    grand_total = jnp.sum(marg_float)
    log_margins = jnp.log(marg_float)
    row_logs = lax.dynamic_index_in_dim(
        log_margins.reshape(col_count, row_count, terms_here), row_index, 1, keepdims=False
    )
    col_logs = lax.dynamic_slice_in_dim(log_margins, col_index * group_size, group_size).reshape(
        -1, tile_size
    )
    log_ratio = (
        jnp.log(jnp.maximum(tile_counts.astype(jnp.float32), 1.0))
        + jnp.log(grand_total)
        - jnp.take(row_logs, tile_rows, axis=0)[:, :, None]
        - jnp.take(col_logs, tile_cols, axis=0)[:, None, :]
    )
    position = jnp.arange(capacity, dtype=jnp.int32)
    keep_mask = (tile_counts > 0) & (position < tile_live[0])[:, None, None]
    ppmi = jnp.where(keep_mask, jnp.maximum(log_ratio, 0.0), 0.0).astype(jnp.bfloat16)
    multiply = call(
        multiply_kernel,
        jax.ShapeDtypeStruct((col_count, width_k, terms_here), jnp.float32),
        [SMEM, SMEM, SMEM, VMEM, VMEM],
    )
    solve = call(
        solve_kernel,
        jax.ShapeDtypeStruct((width_k, terms_here), jnp.float32),
        [SMEM, VMEM, VMEM, VMEM],
        [pltpu.VMEM((len(PAIRS), TILE, TILE), jnp.float32), pltpu.VMEM((TILE, TILE), jnp.float32)],
    )
    for sweep_index in range(ITERS):
        if sweep_index:
            gathered = lax.all_gather(current.astype(jnp.bfloat16), ROWS, axis=0)
        partial_sum = multiply(tile_live, tile_rows, tile_cols, gathered, ppmi)
        image = lax.psum_scatter(partial_sum, "z", scatter_dimension=0)
        own, other = gram_sum(core, image)
        current = solve(core, own, other, image)
    return current


def solution(mesh):
    rows, cols = mesh.shape["rows"], mesh.shape["cols"]
    side = 4
    devices = mesh.devices.reshape(side, rows // (2 * side), 2, cols)
    inner = Mesh(devices, ("x", "y", "core", "z"))
    lists = (*ROWS, "z")
    terms = ("z", *ROWS)
    in_specs = (P(None, terms), P(lists, None, None), P(lists), P(lists), P(lists), P())
    return jax.shard_map(
        local, mesh=inner, in_specs=in_specs, out_specs=P(None, terms), check_vma=False
    )
```

```python
import jax
import jax.numpy as jnp
from jax import lax
from jax.experimental import pallas as pl
from jax.experimental.pallas import tpu as pltpu
from jax.sharding import Mesh, PartitionSpec as P

ITERS = 2
HIGHEST = lax.Precision.HIGHEST
TILE = 128
SUB = 8
BLOCKS = 4
PAIRS = [(i, j) for i in range(BLOCKS) for j in range(i + 1)]
PLACE = {pair: n for n, pair in enumerate(PAIRS)}
HALF = len(PAIRS) // 2
ROWS = ("x", "y", "core")
PLANE = ("x", "y")
VMEM = pl.BlockSpec(memory_space=pltpu.VMEM)
SMEM = pl.BlockSpec(memory_space=pltpu.SMEM)


def dot_nt(a, b, precision=HIGHEST):
    return lax.dot_general(
        a, b, (((1,), (1,)), ((), ())), precision=precision, preferred_element_type=jnp.float32
    )


def dot_nn(a, b):
    return jnp.dot(a, b, precision=HIGHEST, preferred_element_type=jnp.float32)


def call(kernel, out_shape, in_specs, scratch=(), mib=16):
    return pl.pallas_call(
        kernel,
        out_shape=out_shape,
        in_specs=in_specs,
        out_specs=VMEM,
        scratch_shapes=list(scratch),
        compiler_params=pltpu.CompilerParams(vmem_limit_bytes=mib * 1024 * 1024),
    )


def multiply_kernel(live_ref, rows_ref, cols_ref, basis_ref, ppmi_ref, out_ref):
    out_ref[...] = jnp.zeros_like(out_ref)

    def add_tile(t, carry):
        r = rows_ref[t]
        product = dot_nt(basis_ref[cols_ref[t]], ppmi_ref[t], None)
        out_ref[r] = out_ref[r] + product
        return carry

    lax.fori_loop(0, live_ref[0], add_tile, 0)


def apply_multiply_kernel(
    live_ref, rows_ref, cols_ref, pairs_ref, used_ref, inverse_ref, image_ref, ppmi_ref, out_ref,
    top_ref, low_ref, wide_ref, basis_ref,
):
    half = inverse_ref.shape[0] // 2

    def split(x):
        high = x.astype(jnp.bfloat16)
        return high, (x - high.astype(jnp.float32)).astype(jnp.bfloat16)

    for target, rows, depth in ((top_ref, 0, half), (low_ref, half, 2 * half)):
        high, rest = split(inverse_ref[pl.ds(rows, half), pl.ds(0, depth)])
        for k in range(depth // half):
            part = slice(k * half, (k + 1) * half)
            for n, piece in enumerate((high, high, rest)):
                target[:, pl.ds((3 * k + n) * half, half)] = piece[:, part]

    def add_columns(k, carry):
        first, second = used_ref[2 * k], used_ref[2 * k + 1]
        for side, c in enumerate((first, second)):
            lanes = pl.ds(side * TILE, TILE)
            for part in range(2):
                high, rest = split(image_ref[c, pl.ds(part * half, half), :])
                for n, piece in enumerate((high, rest, high)):
                    wide_ref[pl.ds((3 * part + n) * half, half), lanes] = piece
        for rows, source, depth in ((0, top_ref, 3 * half), (half, low_ref, 6 * half)):
            product = jnp.dot(
                source[...], wide_ref[pl.ds(0, depth), :], preferred_element_type=jnp.float32
            ).astype(jnp.bfloat16)
            basis_ref[first, pl.ds(rows, half), :] = product[:, :TILE]
            basis_ref[second, pl.ds(rows, half), :] = product[:, TILE:]
        return carry

    lax.fori_loop(0, pairs_ref[0], add_columns, 0)
    multiply_kernel(live_ref, rows_ref, cols_ref, basis_ref, ppmi_ref, out_ref)


def gram_kernel(core_ref, own_ref, other_ref, out_ref):
    for n in range(HALF):
        first, second = PAIRS[n], PAIRS[HALF + n]
        core = core_ref[0]
        i = pl.multiple_of(jnp.where(core == 0, first[0], second[0]) * TILE, TILE)
        j = pl.multiple_of(jnp.where(core == 0, first[1], second[1]) * TILE, TILE)
        out_ref[n] = dot_nt(own_ref[pl.ds(i, TILE), :], own_ref[pl.ds(j, TILE), :]) + dot_nt(
            other_ref[pl.ds(i, TILE), :], other_ref[pl.ds(j, TILE), :]
        )


def spread_row(x, m):
    return jnp.broadcast_to(x[m : m + 1, :], (SUB, TILE))


def spread_col(x, lane):
    return jnp.broadcast_to(x[:, lane : lane + 1], (SUB, TILE))


def factor_inverse(read, write):
    n = TILE // SUB
    a = [read(i) for i in range(n)]
    row = lax.broadcasted_iota(jnp.int32, (SUB, TILE), 0)
    lane = lax.broadcasted_iota(jnp.int32, (SUB, TILE), 1)
    m = [jnp.where(lane == row + SUB * i, 1.0, 0.0).astype(jnp.float32) for i in range(n)]
    for p in range(n):
        cols = [[spread_col(a[i], SUB * p + k) for i in range(p, n)] for k in range(SUB)]
        s = [[spread_row(cols[k][0], q) if q >= k else None for k in range(SUB)] for q in range(SUB)]
        u = [spread_row(a[p], k) for k in range(SUB)]
        v = [spread_row(m[p], k) for k in range(SUB)]
        following = [cols[k][1] for k in range(SUB)] if p + 1 < n else None
        low = [[None] * SUB for _ in range(SUB)]
        root = [None] * SUB
        for k in range(SUB):
            root[k] = lax.rsqrt(s[k][k])
            for q in range(k + 1, SUB):
                low[q][k] = s[q][k] * root[k]
            for q in range(k + 1, SUB):
                for t in range(k + 1, q + 1):
                    s[q][t] = s[q][t] - low[q][k] * low[t][k]
            u[k] = u[k] * root[k]
            v[k] = v[k] * root[k]
            for q in range(k + 1, SUB):
                u[q] = u[q] - low[q][k] * u[k]
                v[q] = v[q] - low[q][k] * v[k]
            if following is not None:
                following[k] = following[k] * root[k]
                for q in range(k + 1, SUB):
                    following[q] = following[q] - low[q][k] * following[k]
        for k in range(SUB):
            write(SUB * p + k, v[k])
        if p + 1 == n:
            break
        for k in range(SUB):
            a[p + 1] = a[p + 1] - following[k] * u[k]
        zu = [None] * SUB
        zv = [None] * SUB
        for k in reversed(range(SUB)):
            x, y = u[k], v[k]
            for q in range(k + 1, SUB):
                x = x - low[q][k] * zu[q]
                y = y - low[q][k] * zv[q]
            zu[k] = x * root[k]
            zv[k] = y * root[k]
        for i in range(p + 1, n):
            for k in range(SUB):
                if i > p + 1:
                    a[i] = a[i] - cols[k][i - p] * zu[k]
                m[i] = m[i] - cols[k][i - p] * zv[k]


def factorize(core_ref, own_ref, other_ref, a_ref, w_ref, step):
    core = core_ref[0]
    for n in range(HALF):
        a_ref[core * HALF + n] = own_ref[n]
        a_ref[(1 - core) * HALF + n] = other_ref[n]
    factor = {}
    for j in range(BLOCKS):
        here = PLACE[j, j]

        def read(i):
            return a_ref[here, pl.ds(SUB * i, SUB), :]

        def write(r, value):
            w_ref[pl.ds(r, 1), :] = value[0:1, :]

        factor_inverse(read, write)
        inverse = w_ref[...]
        for i in range(j + 1, BLOCKS):
            factor[i, j] = dot_nt(a_ref[PLACE[i, j]], inverse)
        for i in range(j + 1, BLOCKS):
            for k in range(j + 1, i + 1):
                n = PLACE[i, k]
                a_ref[n] = a_ref[n] - dot_nt(factor[i, j], factor[k, j])
        step(j, factor, inverse)


def solve_kernel(core_ref, own_ref, other_ref, image_ref, out_ref, a_ref, w_ref):
    solved = []

    def step(j, factor, inverse):
        rest = image_ref[pl.ds(TILE * j, TILE), :]
        for i in range(j):
            rest = rest - dot_nn(factor[j, i], solved[i])
        solved.append(dot_nn(inverse, rest))
        out_ref[pl.ds(TILE * j, TILE), :] = solved[j]

    factorize(core_ref, own_ref, other_ref, a_ref, w_ref, step)


def inverse_kernel(core_ref, own_ref, other_ref, out_ref, a_ref, w_ref):
    out_ref[...] = jnp.zeros_like(out_ref)

    def step(j, factor, inverse):
        here = pl.ds(TILE * j, TILE)
        out_ref[here, here] = inverse
        if j:
            rest = jnp.zeros((TILE, TILE * j), jnp.float32)
            for k in range(j):
                rest = rest - dot_nn(factor[j, k], out_ref[pl.ds(TILE * k, TILE), pl.ds(0, TILE * j)])
            out_ref[here, pl.ds(0, TILE * j)] = dot_nn(inverse, rest)

    factorize(core_ref, own_ref, other_ref, a_ref, w_ref, step)


def swap_core(x):
    return lax.ppermute(x, "core", [(0, 1), (1, 0)])


def gram_sum(core, image):
    k, width = image.shape
    plane = lax.axis_size(PLANE)
    depth = lax.axis_size("z")
    part = call(
        gram_kernel, jax.ShapeDtypeStruct((HALF, TILE, TILE), jnp.float32), [SMEM, VMEM, VMEM]
    )(core, image, swap_core(image))
    part = part.reshape(plane, HALF * TILE // plane, TILE)
    part = jnp.sum(lax.all_to_all(part, PLANE, 0, 0), axis=0)
    part = jnp.broadcast_to(part[None], (depth,) + part.shape)
    part = jnp.sum(lax.all_to_all(part, "z", 0, 0), axis=0)
    part = jnp.broadcast_to(part[None], (plane,) + part.shape)
    part = lax.all_to_all(part, PLANE, 0, 0)
    part = part.reshape(HALF, TILE, TILE)
    return part, swap_core(part)


def local(basis, tile_counts, tile_rows, tile_cols, tile_live, marginals):
    width_k, terms_here = basis.shape
    capacity, tile_size, _ = tile_counts.shape
    row_count = lax.axis_size(ROWS)
    col_count = lax.axis_size("z")
    row_index = lax.axis_index(ROWS)
    col_index = lax.axis_index("z")
    core = lax.axis_index("core").astype(jnp.int32).reshape(1)
    group_size = row_count * terms_here
    gathered = lax.all_gather(basis.astype(jnp.bfloat16), ROWS, axis=0)
    marg_float = marginals.astype(jnp.float32)
    grand_total = jnp.sum(marg_float)
    log_margins = jnp.log(marg_float)
    row_logs = lax.dynamic_index_in_dim(
        log_margins.reshape(col_count, row_count, terms_here), row_index, 1, keepdims=False
    )
    col_logs = lax.dynamic_slice_in_dim(log_margins, col_index * group_size, group_size).reshape(
        -1, tile_size
    )
    log_ratio = (
        jnp.log(jnp.maximum(tile_counts.astype(jnp.float32), 1.0))
        + jnp.log(grand_total)
        - jnp.take(row_logs, tile_rows, axis=0)[:, :, None]
        - jnp.take(col_logs, tile_cols, axis=0)[:, None, :]
    )
    position = jnp.arange(capacity, dtype=jnp.int32)
    keep_mask = (tile_counts > 0) & (position < tile_live[0])[:, None, None]
    ppmi = jnp.where(keep_mask, jnp.maximum(log_ratio, 0.0), 0.0).astype(jnp.bfloat16)
    column = jnp.arange(row_count, dtype=jnp.int32)
    live = (position < tile_live[0])[:, None]
    needed = jnp.any((tile_cols[:, None] == column[None, :]) & live, axis=0)
    rank = jnp.sum((needed[None, :] & (column[None, :] < column[:, None])).astype(jnp.int32), axis=1)
    placed = needed[None, :] & (rank[None, :] == column[:, None])
    used = jnp.sum(jnp.where(placed, column[None, :], 0), axis=1)
    pairs = ((jnp.sum(needed.astype(jnp.int32)) + 1) // 2).reshape(1)
    image_parts = jax.ShapeDtypeStruct((col_count, width_k, terms_here), jnp.float32)
    half = width_k // 2
    multiply = call(multiply_kernel, image_parts, [SMEM] * 3 + [VMEM] * 2)
    apply_multiply = call(
        apply_multiply_kernel,
        image_parts,
        [SMEM] * 5 + [VMEM] * 3,
        [
            pltpu.VMEM((half, 3 * half), jnp.bfloat16),
            pltpu.VMEM((half, 6 * half), jnp.bfloat16),
            pltpu.VMEM((6 * half, 2 * TILE), jnp.bfloat16),
            pltpu.VMEM((row_count, width_k, terms_here), jnp.bfloat16),
        ],
        mib=32,
    )
    scratch = [
        pltpu.VMEM((len(PAIRS), TILE, TILE), jnp.float32),
        pltpu.VMEM((TILE, TILE), jnp.float32),
    ]
    invert = call(
        inverse_kernel,
        jax.ShapeDtypeStruct((width_k, width_k), jnp.float32),
        [SMEM, VMEM, VMEM],
        scratch,
    )
    solve = call(
        solve_kernel,
        jax.ShapeDtypeStruct((width_k, terms_here), jnp.float32),
        [SMEM, VMEM, VMEM, VMEM],
        scratch,
    )
    places = (tile_live, tile_rows, tile_cols)
    for sweep_index in range(ITERS):
        if sweep_index:
            partial_sum = apply_multiply(*places, pairs, used, inverse, gathered, ppmi)
        else:
            partial_sum = multiply(*places, gathered, ppmi)
        image = lax.psum_scatter(partial_sum, "z", scatter_dimension=0)
        last = sweep_index + 1 == ITERS
        if not last:
            gathered = lax.all_gather(image, ROWS, axis=0)
        own, other = gram_sum(core, image)
        if not last:
            inverse = invert(core, own, other)
    return solve(core, own, other, image)


def solution(mesh):
    rows, cols = mesh.shape["rows"], mesh.shape["cols"]
    side = 4
    devices = mesh.devices.reshape(side, rows // (2 * side), 2, cols)
    inner = Mesh(devices, ("x", "y", "core", "z"))
    lists = (*ROWS, "z")
    terms = ("z", *ROWS)
    in_specs = (P(None, terms), P(lists, None, None), P(lists), P(lists), P(lists), P())
    return jax.shard_map(
        local, mesh=inner, in_specs=in_specs, out_specs=P(None, terms), check_vma=False
    )
```

```python
import functools

import jax
import jax.numpy as jnp
from jax import lax
from jax.experimental import pallas as pl
from jax.experimental.pallas import tpu as pltpu
from jax.sharding import Mesh, PartitionSpec as P

HIGHEST = lax.Precision.HIGHEST
TILE = 128
SUB = 8
BLOCKS = 4
PAIRS = [(i, j) for i in range(BLOCKS) for j in range(i + 1)]
PLACE = {pair: n for n, pair in enumerate(PAIRS)}
HALF = len(PAIRS) // 2
FAR = 4
ROWS = ("x", "y", "core")
PLANE = ("x", "y")
VMEM = pl.BlockSpec(memory_space=pltpu.VMEM)
ANY = pl.BlockSpec(memory_space=pl.ANY)
SMEM = pl.BlockSpec(memory_space=pltpu.SMEM)


def dot_nt(a, b, precision=HIGHEST):
    return lax.dot_general(
        a, b, (((1,), (1,)), ((), ())), precision=precision, preferred_element_type=jnp.float32
    )


def dot_nn(a, b):
    return jnp.dot(a, b, precision=HIGHEST, preferred_element_type=jnp.float32)


def call(kernel, out_shape, in_specs, scratch=(), mib=16, flops=0):
    return pl.pallas_call(
        kernel,
        out_shape=out_shape,
        in_specs=in_specs,
        out_specs=jax.tree.map(lambda shape: VMEM, out_shape),
        scratch_shapes=list(scratch),
        compiler_params=pltpu.CompilerParams(vmem_limit_bytes=mib * 1024 * 1024),
        cost_estimate=pl.CostEstimate(flops=flops, bytes_accessed=2**22, transcendentals=0),
    )


def multiply(farthest, place_ref, rows_ref, cols_ref, basis_ref, ppmi_ref, out_ref):
    out_ref[...] = jnp.zeros_like(out_ref)
    half = out_ref.shape[1]

    def add_tile(t, carry):
        distance = rows_ref[t]

        @pl.when((distance == FAR) == farthest)
        def _():
            product = dot_nt(basis_ref[cols_ref[t]], ppmi_ref[t], None)
            if farthest:
                for n in range(2):
                    out_ref[n] = out_ref[n] + product[n * half : (n + 1) * half]
            else:
                out_ref[distance] = out_ref[distance] + product

        return carry

    lax.fori_loop(0, place_ref[0], add_tile, 0)


def multiply_kernel(farthest, live_ref, rows_ref, cols_ref, ppmi_ref, *refs):
    *pieces, out_ref, basis_ref, sems = refs
    size = pieces[0].shape[0]
    copies = [
        pltpu.make_async_copy(piece, basis_ref.at[pl.ds(n * size, size)], sems.at[n])
        for n, piece in enumerate(pieces)
    ]
    for copy in copies:
        copy.start()
    for copy in copies:
        copy.wait()
    multiply(farthest, live_ref, rows_ref, cols_ref, basis_ref, ppmi_ref, out_ref)


def split(x):
    high = x.astype(jnp.bfloat16)
    return high, (x - high.astype(jnp.float32)).astype(jnp.bfloat16)


def apply_multiply_kernel(
    farthest, live_ref, rows_ref, cols_ref, pairs_ref, used_ref, top_ref, low_ref, image_ref, ppmi_ref,
    out_ref, columns_ref, wide_ref, basis_ref, sems,
):
    half = top_ref.shape[0]
    pairs = pairs_ref[0]

    def fetch(k, slot):
        return [
            pltpu.make_async_copy(
                image_ref.at[used_ref[2 * k + side]], columns_ref.at[slot, side], sems.at[slot, side]
            )
            for side in range(2)
        ]

    @pl.when(pairs > 0)
    def _():
        for copy in fetch(0, 0):
            copy.start()

    def add_columns(k, carry):
        slot = lax.rem(k, 2)

        @pl.when(k + 1 < pairs)
        def _():
            for copy in fetch(k + 1, 1 - slot):
                copy.start()

        for copy in fetch(k, slot):
            copy.wait()
        for side in range(2):
            lanes = pl.ds(side * TILE, TILE)
            for part in range(2):
                high, rest = split(columns_ref[slot, side, pl.ds(part * half, half), :])
                for n, piece in enumerate((high, rest, high)):
                    wide_ref[pl.ds((3 * part + n) * half, half), lanes] = piece
        for rows, source, depth in ((0, top_ref, 3 * half), (half, low_ref, 6 * half)):
            product = jnp.dot(
                source[...], wide_ref[pl.ds(0, depth), :], preferred_element_type=jnp.float32
            ).astype(jnp.bfloat16)
            basis_ref[used_ref[2 * k], pl.ds(rows, half), :] = product[:, :TILE]
            basis_ref[used_ref[2 * k + 1], pl.ds(rows, half), :] = product[:, TILE:]
        return carry

    lax.fori_loop(0, pairs, add_columns, 0)
    multiply(farthest, live_ref, rows_ref, cols_ref, basis_ref, ppmi_ref, out_ref)


def gram_kernel(core_ref, own_ref, other_ref, out_ref):
    for n in range(HALF):
        first, second = PAIRS[n], PAIRS[HALF + n]
        core = core_ref[0]
        i = pl.multiple_of(jnp.where(core == 0, first[0], second[0]) * TILE, TILE)
        j = pl.multiple_of(jnp.where(core == 0, first[1], second[1]) * TILE, TILE)
        out_ref[n] = dot_nt(own_ref[pl.ds(i, TILE), :], own_ref[pl.ds(j, TILE), :]) + dot_nt(
            other_ref[pl.ds(i, TILE), :], other_ref[pl.ds(j, TILE), :]
        )


def spread_row(x, m):
    return jnp.broadcast_to(x[m : m + 1, :], (SUB, TILE))


def spread_col(x, lane):
    return jnp.broadcast_to(x[:, lane : lane + 1], (SUB, TILE))


def factor_inverse(read, write):
    n = TILE // SUB
    a = [read(i) for i in range(n)]
    row = lax.broadcasted_iota(jnp.int32, (SUB, TILE), 0)
    lane = lax.broadcasted_iota(jnp.int32, (SUB, TILE), 1)
    m = [jnp.where(lane == row + SUB * i, 1.0, 0.0).astype(jnp.float32) for i in range(n)]
    for p in range(n):
        cols = [[spread_col(a[i], SUB * p + k) for i in range(p, n)] for k in range(SUB)]
        s = [[spread_row(cols[k][0], q) if q >= k else None for k in range(SUB)] for q in range(SUB)]
        u = [spread_row(a[p], k) for k in range(SUB)]
        v = [spread_row(m[p], k) for k in range(SUB)]
        following = [cols[k][1] for k in range(SUB)] if p + 1 < n else None
        low = [[None] * SUB for _ in range(SUB)]
        root = [None] * SUB
        for k in range(SUB):
            root[k] = lax.rsqrt(s[k][k])
            for q in range(k + 1, SUB):
                low[q][k] = s[q][k] * root[k]
            for q in range(k + 1, SUB):
                for t in range(k + 1, q + 1):
                    s[q][t] = s[q][t] - low[q][k] * low[t][k]
            u[k] = u[k] * root[k]
            v[k] = v[k] * root[k]
            for q in range(k + 1, SUB):
                u[q] = u[q] - low[q][k] * u[k]
                v[q] = v[q] - low[q][k] * v[k]
            if following is not None:
                following[k] = following[k] * root[k]
                for q in range(k + 1, SUB):
                    following[q] = following[q] - low[q][k] * following[k]
        for k in range(SUB):
            write(SUB * p + k, v[k])
        if p + 1 == n:
            break
        for k in range(SUB):
            a[p + 1] = a[p + 1] - following[k] * u[k]
        zu = [None] * SUB
        zv = [None] * SUB
        for k in reversed(range(SUB)):
            x, y = u[k], v[k]
            for q in range(k + 1, SUB):
                x = x - low[q][k] * zu[q]
                y = y - low[q][k] * zv[q]
            zu[k] = x * root[k]
            zv[k] = y * root[k]
        for i in range(p + 1, n):
            for k in range(SUB):
                if i > p + 1:
                    a[i] = a[i] - cols[k][i - p] * zu[k]
                m[i] = m[i] - cols[k][i - p] * zv[k]


def factorize(core_ref, own_ref, other_ref, a_ref, w_ref, step):
    core = core_ref[0]
    for n in range(HALF):
        a_ref[core * HALF + n] = own_ref[n]
        a_ref[(1 - core) * HALF + n] = other_ref[n]
    factor = {}
    for j in range(BLOCKS):
        here = PLACE[j, j]

        def read(i):
            return a_ref[here, pl.ds(SUB * i, SUB), :]

        def write(r, value):
            w_ref[pl.ds(r, 1), :] = value[0:1, :]

        factor_inverse(read, write)
        inverse = w_ref[...]
        for i in range(j + 1, BLOCKS):
            factor[i, j] = dot_nt(a_ref[PLACE[i, j]], inverse)
        for i in range(j + 1, BLOCKS):
            for k in range(j + 1, i + 1):
                n = PLACE[i, k]
                a_ref[n] = a_ref[n] - dot_nt(factor[i, j], factor[k, j])
        step(j, factor, inverse)


def solve_kernel(core_ref, own_ref, other_ref, image_ref, out_ref, a_ref, w_ref):
    solved = []

    def step(j, factor, inverse):
        rest = image_ref[pl.ds(TILE * j, TILE), :]
        for i in range(j):
            rest = rest - dot_nn(factor[j, i], solved[i])
        solved.append(dot_nn(inverse, rest))
        out_ref[pl.ds(TILE * j, TILE), :] = solved[j]

    factorize(core_ref, own_ref, other_ref, a_ref, w_ref, step)


def inverse_kernel(core_ref, own_ref, other_ref, top_ref, low_ref, a_ref, w_ref, x_ref):
    x_ref[...] = jnp.zeros_like(x_ref)

    def step(j, factor, inverse):
        here = pl.ds(TILE * j, TILE)
        x_ref[here, here] = inverse
        if j:
            rest = jnp.zeros((TILE, TILE * j), jnp.float32)
            for k in range(j):
                rest = rest - dot_nn(factor[j, k], x_ref[pl.ds(TILE * k, TILE), pl.ds(0, TILE * j)])
            x_ref[here, pl.ds(0, TILE * j)] = dot_nn(inverse, rest)

    factorize(core_ref, own_ref, other_ref, a_ref, w_ref, step)
    half = top_ref.shape[0]
    for target, rows, parts in ((top_ref, 0, 1), (low_ref, half, 2)):
        for k in range(parts):
            high, rest = split(x_ref[pl.ds(rows, half), pl.ds(k * half, half)])
            for n, piece in enumerate((high, high, rest)):
                target[:, pl.ds((3 * k + n) * half, half)] = piece


def swap_core(x):
    return lax.ppermute(x, "core", [(0, 1), (1, 0)])


def shift(x, step, turned):
    side_x, side_y = lax.axis_size("x"), lax.axis_size("y")
    pairs = []
    for i in range(side_x):
        for j in range(side_y):
            for core in range(2):
                to = (i + step) % side_x, j
                if turned != bool(core):
                    to = i, (j + step) % side_y
                pairs.append(((i * side_y + j) * 2 + core, (to[0] * side_y + to[1]) * 2 + core))
    return lax.ppermute(x, ROWS, pairs)


def gather_lines(x):
    line = jnp.stack([x] + [shift(x, step, False) for step in (1, 2, 3)])
    lines = [line] + [shift(line, step, True) for step in (1, 2, 3)]
    return lines + [swap_core(line) for line in lines]


def line_slot(column):
    core = column % 2
    along_x = (lax.axis_index("x") - column // 8) % 4
    along_y = (lax.axis_index("y") - column // 2 % 4) % 4
    inside = jnp.where(core == 0, along_y * 4 + along_x, along_x * 4 + along_y)
    return inside + jnp.where(core == lax.axis_index("core"), 0, 16)


def ring_sum(far, parts):
    size = lax.axis_size("z")

    def up(x):
        return lax.ppermute(x, "z", [(i, (i + 1) % size) for i in range(size)])

    def down(x):
        return lax.ppermute(x, "z", [((i + 1) % size, i) for i in range(size)])

    half = far.shape[1]
    right = jnp.pad(up(far[0]), ((0, half), (0, 0)))
    left = jnp.pad(down(far[1]), ((half, 0), (0, 0)))
    for step in range(1, FAR):
        sums = lax.optimization_barrier((parts[FAR - step] + right, parts[FAR + step] + left))
        right, left = up(sums[0]), down(sums[1])
    return parts[0] + right + left


def gram_sum(core, image):
    k, width = image.shape
    plane = lax.axis_size(PLANE)
    depth = lax.axis_size("z")
    part = call(
        gram_kernel, jax.ShapeDtypeStruct((HALF, TILE, TILE), jnp.float32), [SMEM, VMEM, VMEM]
    )(core, image, swap_core(image))
    part = part.reshape(plane, HALF * TILE // plane, TILE)
    part = jnp.sum(lax.all_to_all(part, PLANE, 0, 0), axis=0)
    part = jnp.broadcast_to(part[None], (depth,) + part.shape)
    part = jnp.sum(lax.all_to_all(part, "z", 0, 0), axis=0)
    part = jnp.broadcast_to(part[None], (plane,) + part.shape)
    part = lax.all_to_all(part, PLANE, 0, 0)
    part = part.reshape(HALF, TILE, TILE)
    return part, swap_core(part)


def local(basis, tile_counts, tile_rows, tile_cols, tile_live, marginals):
    width_k, terms_here = basis.shape
    capacity, tile_size, _ = tile_counts.shape
    row_count = lax.axis_size(ROWS)
    col_count = lax.axis_size("z")
    row_index = lax.axis_index(ROWS)
    col_index = lax.axis_index("z")
    core = lax.axis_index("core").astype(jnp.int32).reshape(1)
    group_size = row_count * terms_here
    lines = gather_lines(basis.astype(jnp.bfloat16))
    marg_float = marginals.astype(jnp.float32)
    grand_total = jnp.sum(marg_float)
    log_margins = jnp.log(marg_float)
    row_logs = lax.dynamic_index_in_dim(
        log_margins.reshape(col_count, row_count, terms_here), row_index, 1, keepdims=False
    )
    col_logs = lax.dynamic_slice_in_dim(log_margins, col_index * group_size, group_size).reshape(
        -1, tile_size
    )
    log_ratio = (
        jnp.log(jnp.maximum(tile_counts.astype(jnp.float32), 1.0))
        + jnp.log(grand_total)
        - jnp.take(row_logs, tile_rows, axis=0)[:, :, None]
        - jnp.take(col_logs, tile_cols, axis=0)[:, None, :]
    )
    position = jnp.arange(capacity, dtype=jnp.int32)
    keep_mask = (tile_counts > 0) & (position < tile_live[0])[:, None, None]
    ppmi = jnp.where(keep_mask, jnp.maximum(log_ratio, 0.0), 0.0).astype(jnp.bfloat16)
    distance = (tile_rows - col_index) % col_count
    column = jnp.arange(row_count, dtype=jnp.int32)

    def used_columns(chosen):
        chosen = chosen & (position < tile_live[0])
        needed = jnp.any((tile_cols[:, None] == column[None, :]) & chosen[:, None], axis=0)
        rank = jnp.sum((needed[None, :] & (column[None, :] < column[:, None])).astype(jnp.int32), axis=1)
        placed = needed[:, None] & (rank[:, None] == column[None, :])
        used = jnp.sum(jnp.where(placed, column[:, None], 0), axis=0)
        return ((jnp.sum(needed.astype(jnp.int32)) + 1) // 2).reshape(1), used

    half = width_k // 2
    basis_scratch = pltpu.VMEM((row_count, width_k, terms_here), jnp.bfloat16)
    shapes = {
        True: jax.ShapeDtypeStruct((2, half, terms_here), jnp.float32),
        False: jax.ShapeDtypeStruct((col_count, width_k, terms_here), jnp.float32),
    }

    def first_product(farthest):
        return call(
            functools.partial(multiply_kernel, farthest),
            shapes[farthest],
            [SMEM] * 3 + [VMEM] + [ANY] * len(lines),
            [basis_scratch, pltpu.SemaphoreType.DMA((len(lines),))],
            flops=2**30 if farthest else 2**32,
        )(tile_live, distance, line_slot(tile_cols), ppmi, *lines)

    def second_product(farthest, top, low, gathered):
        pairs, used = used_columns((distance == FAR) == farthest)
        return call(
            functools.partial(apply_multiply_kernel, farthest),
            shapes[farthest],
            [SMEM] * 5 + [VMEM] * 2 + [ANY, VMEM],
            [
                pltpu.VMEM((2, 2, width_k, terms_here), jnp.float32),
                pltpu.VMEM((6 * half, 2 * TILE), jnp.bfloat16),
                basis_scratch,
                pltpu.SemaphoreType.DMA((2, 2)),
            ],
            mib=56,
            flops=2**30 if farthest else 2**32,
        )(tile_live, distance, tile_cols, pairs, used, top, low, gathered, ppmi)

    scratch = [
        pltpu.VMEM((len(PAIRS), TILE, TILE), jnp.float32),
        pltpu.VMEM((TILE, TILE), jnp.float32),
    ]
    invert = call(
        inverse_kernel,
        [
            jax.ShapeDtypeStruct((half, 3 * half), jnp.bfloat16),
            jax.ShapeDtypeStruct((half, 6 * half), jnp.bfloat16),
        ],
        [SMEM, VMEM, VMEM],
        scratch + [pltpu.VMEM((width_k, width_k), jnp.float32)],
    )
    solve = call(
        solve_kernel,
        jax.ShapeDtypeStruct((width_k, terms_here), jnp.float32),
        [SMEM, VMEM, VMEM, VMEM],
        scratch,
    )
    image = ring_sum(first_product(True), first_product(False))
    gathered = lax.all_gather(image, ROWS, axis=0)
    top, low = invert(core, *gram_sum(core, image))
    image = ring_sum(second_product(True, top, low, gathered), second_product(False, top, low, gathered))
    return solve(core, *gram_sum(core, image), image)


def solution(mesh):
    rows, cols = mesh.shape["rows"], mesh.shape["cols"]
    side = 4
    devices = mesh.devices.reshape(side, rows // (2 * side), 2, cols)
    inner = Mesh(devices, ("x", "y", "core", "z"))
    lists = (*ROWS, "z")
    terms = ("z", *ROWS)
    in_specs = (P(None, terms), P(lists, None, None), P(lists), P(lists), P(lists), P())
    return jax.shard_map(
        local, mesh=inner, in_specs=in_specs, out_specs=P(None, terms), check_vma=False
    )
```

```python
import functools

import jax
import jax.numpy as jnp
from jax import lax
from jax.experimental import pallas as pl
from jax.experimental.pallas import tpu as pltpu
from jax.sharding import Mesh, PartitionSpec as P

HIGHEST = lax.Precision.HIGHEST
TILE = 128
SUB = 8
BLOCKS = 4
PAIRS = [(i, j) for i in range(BLOCKS) for j in range(i + 1)]
PLACE = {pair: n for n, pair in enumerate(PAIRS)}
HALF = len(PAIRS) // 2
FAR = 4
ROWS = ("x", "y", "core")
PLANE = ("x", "y")
VMEM = pl.BlockSpec(memory_space=pltpu.VMEM)
ANY = pl.BlockSpec(memory_space=pl.ANY)
SMEM = pl.BlockSpec(memory_space=pltpu.SMEM)


def dot_nt(a, b, precision=HIGHEST):
    return lax.dot_general(
        a, b, (((1,), (1,)), ((), ())), precision=precision, preferred_element_type=jnp.float32
    )


def dot_nn(a, b):
    return jnp.dot(a, b, precision=HIGHEST, preferred_element_type=jnp.float32)


def call(kernel, out_shape, in_specs, scratch=(), mib=16, flops=0):
    return pl.pallas_call(
        kernel,
        out_shape=out_shape,
        in_specs=in_specs,
        out_specs=jax.tree.map(lambda shape: VMEM, out_shape),
        scratch_shapes=list(scratch),
        compiler_params=pltpu.CompilerParams(vmem_limit_bytes=mib * 1024 * 1024),
        cost_estimate=pl.CostEstimate(flops=flops, bytes_accessed=2**22, transcendentals=0),
    )


def multiply_kernel(farthest, count_ref, tiles_ref, rows_ref, cols_ref, ppmi_ref, *refs):
    *pieces, out_ref, basis_ref, sems = refs
    size = pieces[0].shape[0]
    copies = [
        pltpu.make_async_copy(piece, basis_ref.at[pl.ds(n * size, size)], sems.at[n])
        for n, piece in enumerate(pieces)
    ]
    for copy in copies:
        copy.start()
    out_ref[...] = jnp.zeros_like(out_ref)
    for copy in copies:
        copy.wait()

    def add_tile(n, carry):
        t = tiles_ref[n]
        add_product(farthest, out_ref, rows_ref[t], dot_nt(basis_ref[cols_ref[t]], ppmi_ref[t], None))
        return carry

    lax.fori_loop(0, count_ref[0], add_tile, 0)


def add_product(farthest, out_ref, distance, product):
    if farthest:
        half = out_ref.shape[1]
        for n in range(2):
            out_ref[n] = out_ref[n] + product[n * half : (n + 1) * half]
    else:
        out_ref[distance] = out_ref[distance] + product


def image_multiply_kernel(
    farthest, count_ref, tiles_ref, rows_ref, cols_ref, image_ref, ppmi_ref, out_ref, columns_ref, parts_ref, sems
):
    count = count_ref[0]
    depth = columns_ref.shape[0]
    width = columns_ref.shape[1]

    def fetch(n):
        slot = lax.rem(n, depth)
        return pltpu.make_async_copy(
            image_ref.at[cols_ref[tiles_ref[n]]], columns_ref.at[slot], sems.at[slot]
        )

    for n in range(depth - 1):

        @pl.when(n < count)
        def _():
            fetch(n).start()

    out_ref[...] = jnp.zeros_like(out_ref)

    def add_tile(n, carry):
        @pl.when(n + depth - 1 < count)
        def _():
            fetch(n + depth - 1).start()

        fetch(n).wait()
        t = tiles_ref[n]
        column = columns_ref[lax.rem(n, depth)]
        high = column.astype(jnp.bfloat16)
        parts_ref[pl.ds(0, width), :] = high
        parts_ref[pl.ds(width, width), :] = (column - high.astype(jnp.float32)).astype(jnp.bfloat16)
        product = dot_nt(parts_ref[...], ppmi_ref[t], None)
        add_product(farthest, out_ref, rows_ref[t], product[:width] + product[width:])
        return carry

    lax.fori_loop(0, count, add_tile, 0)


def gram_half(core, parts, out_ref):
    for n in range(HALF):
        first, second = PAIRS[n], PAIRS[HALF + n]
        i = pl.multiple_of(jnp.where(core == 0, first[0], second[0]) * TILE, TILE)
        j = pl.multiple_of(jnp.where(core == 0, first[1], second[1]) * TILE, TILE)
        out_ref[n] = sum(dot_nt(ref[pl.ds(i, TILE), :], ref[pl.ds(j, TILE), :]) for ref in parts)


def gram_kernel(core_ref, own_ref, other_ref, out_ref):
    gram_half(core_ref[0], [own_ref, other_ref], out_ref)


def spread_row(x, m):
    return jnp.broadcast_to(x[m : m + 1, :], (SUB, TILE))


def spread_col(x, lane):
    return jnp.broadcast_to(x[:, lane : lane + 1], (SUB, TILE))


def factor_inverse(read, write):
    n = TILE // SUB
    a = [read(i) for i in range(n)]
    row = lax.broadcasted_iota(jnp.int32, (SUB, TILE), 0)
    lane = lax.broadcasted_iota(jnp.int32, (SUB, TILE), 1)
    m = [jnp.where(lane == row + SUB * i, 1.0, 0.0).astype(jnp.float32) for i in range(n)]
    for p in range(n):
        cols = [[spread_col(a[i], SUB * p + k) for i in range(p, n)] for k in range(SUB)]
        s = [[spread_row(cols[k][0], q) if q >= k else None for k in range(SUB)] for q in range(SUB)]
        u = [spread_row(a[p], k) for k in range(SUB)]
        v = [spread_row(m[p], k) for k in range(SUB)]
        following = [cols[k][1] for k in range(SUB)] if p + 1 < n else None
        low = [[None] * SUB for _ in range(SUB)]
        root = [None] * SUB
        for k in range(SUB):
            root[k] = lax.rsqrt(s[k][k])
            for q in range(k + 1, SUB):
                low[q][k] = s[q][k] * root[k]
            for q in range(k + 1, SUB):
                for t in range(k + 1, q + 1):
                    s[q][t] = s[q][t] - low[q][k] * low[t][k]
            u[k] = u[k] * root[k]
            v[k] = v[k] * root[k]
            for q in range(k + 1, SUB):
                u[q] = u[q] - low[q][k] * u[k]
                v[q] = v[q] - low[q][k] * v[k]
            if following is not None:
                following[k] = following[k] * root[k]
                for q in range(k + 1, SUB):
                    following[q] = following[q] - low[q][k] * following[k]
        for k in range(SUB):
            write(SUB * p + k, v[k])
        if p + 1 == n:
            break
        for k in range(SUB):
            a[p + 1] = a[p + 1] - following[k] * u[k]
        zu = [None] * SUB
        zv = [None] * SUB
        for k in reversed(range(SUB)):
            x, y = u[k], v[k]
            for q in range(k + 1, SUB):
                x = x - low[q][k] * zu[q]
                y = y - low[q][k] * zv[q]
            zu[k] = x * root[k]
            zv[k] = y * root[k]
        for i in range(p + 1, n):
            for k in range(SUB):
                if i > p + 1:
                    a[i] = a[i] - cols[k][i - p] * zu[k]
                m[i] = m[i] - cols[k][i - p] * zv[k]


def factorize(core_ref, own_ref, other_ref, a_ref, w_ref, step):
    core = core_ref[0]
    for n in range(HALF):
        a_ref[core * HALF + n] = own_ref[n]
        a_ref[(1 - core) * HALF + n] = other_ref[n]
    factor = {}
    for j in range(BLOCKS):
        here = PLACE[j, j]

        def read(i):
            return a_ref[here, pl.ds(SUB * i, SUB), :]

        def write(r, value):
            w_ref[pl.ds(r, 1), :] = value[0:1, :]

        factor_inverse(read, write)
        inverse = w_ref[...]
        for i in range(j + 1, BLOCKS):
            factor[i, j] = dot_nt(a_ref[PLACE[i, j]], inverse)
        for i in range(j + 1, BLOCKS):
            for k in range(j + 1, i + 1):
                n = PLACE[i, k]
                a_ref[n] = a_ref[n] - dot_nt(factor[i, j], factor[k, j])
        step(j, factor, inverse)


def solve_kernel(core_ref, own_ref, other_ref, image_ref, out_ref, a_ref, w_ref):
    solved = []

    def step(j, factor, inverse):
        rest = image_ref[pl.ds(TILE * j, TILE), :]
        for i in range(j):
            rest = rest - dot_nn(factor[j, i], solved[i])
        solved.append(dot_nn(inverse, rest))
        out_ref[pl.ds(TILE * j, TILE), :] = solved[j]

    factorize(core_ref, own_ref, other_ref, a_ref, w_ref, step)


def step_kernel(j, *refs):
    left = [pair for pair in PAIRS if pair[1] >= j]
    later = [pair for pair in PAIRS if pair[1] > j]
    rest_ref = None
    if j == 0:
        core_ref, own_ref, other_ref, col_ref, rest_ref, w_ref, a_ref = refs
        core = core_ref[0]
        for n in range(HALF):
            a_ref[core * HALF + n] = own_ref[n]
            a_ref[(1 - core) * HALF + n] = other_ref[n]
    elif later:
        a_ref, col_ref, rest_ref, w_ref = refs
    else:
        a_ref, col_ref, w_ref = refs

    def read(i):
        return a_ref[left.index((j, j)), pl.ds(SUB * i, SUB), :]

    def write(r, value):
        w_ref[pl.ds(r, 1), :] = value[0:1, :]

    factor_inverse(read, write)
    inverse = w_ref[...]
    col_ref[0] = inverse
    factor = {i: dot_nt(a_ref[left.index((i, j))], inverse) for i in range(j + 1, BLOCKS)}
    for i in factor:
        col_ref[i - j] = factor[i]
    for n, (i, k) in enumerate(later):
        rest_ref[n] = a_ref[left.index((i, k))] - dot_nt(factor[i], factor[k])


def solve_gram_kernel(core_ref, *refs):
    *cols, own_ref, other_ref, image_ref, out_ref, solved_ref = refs
    width = own_ref.shape[1]
    solved = []
    for j in range(BLOCKS):
        here = pl.ds(TILE * j, TILE)
        rest = jnp.concatenate([own_ref[here, :], other_ref[here, :]], axis=1)
        for i in range(j):
            rest = rest - dot_nn(cols[i][j - i], solved[i])
        solved.append(dot_nn(cols[j][0], rest))
        solved_ref[here, :] = solved[j]
        image_ref[here, :] = solved[j][:, :width]
    gram_half(core_ref[0], [solved_ref], out_ref)


def swap_core(x):
    return lax.ppermute(x, "core", [(0, 1), (1, 0)])


def shift(x, step, turned):
    side_x, side_y = lax.axis_size("x"), lax.axis_size("y")
    pairs = []
    for i in range(side_x):
        for j in range(side_y):
            for core in range(2):
                to = (i + step) % side_x, j
                if turned != bool(core):
                    to = i, (j + step) % side_y
                pairs.append(((i * side_y + j) * 2 + core, (to[0] * side_y + to[1]) * 2 + core))
    return lax.ppermute(x, ROWS, pairs)


def gather_lines(x):
    line = jnp.stack([x] + [shift(x, step, False) for step in (1, 2, 3)])
    lines = [line] + [shift(line, step, True) for step in (1, 2, 3)]
    return lines + [swap_core(line) for line in lines]


def line_slot(column):
    core = column % 2
    along_x = (lax.axis_index("x") - column // 8) % 4
    along_y = (lax.axis_index("y") - column // 2 % 4) % 4
    inside = jnp.where(core == 0, along_y * 4 + along_x, along_x * 4 + along_y)
    return inside + jnp.where(core == lax.axis_index("core"), 0, 16)


def ring_sum(far, parts, work=(), state=()):
    size = lax.axis_size("z")

    def up(x):
        return lax.ppermute(x, "z", [(i, (i + 1) % size) for i in range(size)])

    def down(x):
        return lax.ppermute(x, "z", [((i + 1) % size, i) for i in range(size)])

    half = far.shape[1]
    right = jnp.pad(up(far[0]), ((0, half), (0, 0)))
    left = jnp.pad(down(far[1]), ((half, 0), (0, 0)))
    for step in range(1, FAR):
        right, left, state = lax.optimization_barrier(
            (parts[FAR - step] + right, parts[FAR + step] + left, state)
        )
        right, left = up(right), down(left)
        if work:
            state = work[step - 1](state)
            right, left, state = lax.optimization_barrier((right, left, state))
    return parts[0] + right + left, state


def gram_sum(part):
    plane = lax.axis_size(PLANE)
    depth = lax.axis_size("z")
    part = part.reshape(plane, HALF * TILE // plane, TILE)
    part = jnp.sum(lax.all_to_all(part, PLANE, 0, 0), axis=0)
    part = jnp.broadcast_to(part[None], (depth,) + part.shape)
    part = jnp.sum(lax.all_to_all(part, "z", 0, 0), axis=0)
    part = jnp.broadcast_to(part[None], (plane,) + part.shape)
    part = lax.all_to_all(part, PLANE, 0, 0)
    part = part.reshape(HALF, TILE, TILE)
    return part, swap_core(part)


def local(basis, tile_counts, tile_rows, tile_cols, tile_live, marginals):
    width_k, terms_here = basis.shape
    capacity, tile_size, _ = tile_counts.shape
    row_count = lax.axis_size(ROWS)
    col_count = lax.axis_size("z")
    row_index = lax.axis_index(ROWS)
    col_index = lax.axis_index("z")
    core = lax.axis_index("core").astype(jnp.int32).reshape(1)
    group_size = row_count * terms_here
    lines = gather_lines(basis.astype(jnp.bfloat16))
    marg_float = marginals.astype(jnp.float32)
    grand_total = jnp.sum(marg_float)
    log_margins = jnp.log(marg_float)
    row_logs = lax.dynamic_index_in_dim(
        log_margins.reshape(col_count, row_count, terms_here), row_index, 1, keepdims=False
    )
    col_logs = lax.dynamic_slice_in_dim(log_margins, col_index * group_size, group_size).reshape(
        -1, tile_size
    )
    log_ratio = (
        jnp.log(jnp.maximum(tile_counts.astype(jnp.float32), 1.0))
        + jnp.log(grand_total)
        - jnp.take(row_logs, tile_rows, axis=0)[:, :, None]
        - jnp.take(col_logs, tile_cols, axis=0)[:, None, :]
    )
    position = jnp.arange(capacity, dtype=jnp.int32)
    keep_mask = (tile_counts > 0) & (position < tile_live[0])[:, None, None]
    ppmi = jnp.where(keep_mask, jnp.maximum(log_ratio, 0.0), 0.0).astype(jnp.bfloat16)
    distance = (tile_rows - col_index) % col_count

    def listed(chosen):
        chosen = chosen & (position < tile_live[0])
        rank = jnp.sum((chosen[None, :] & (position[None, :] < position[:, None])).astype(jnp.int32), axis=1)
        placed = chosen[:, None] & (rank[:, None] == position[None, :])
        tiles = jnp.sum(jnp.where(placed, position[:, None], 0), axis=0)
        return jnp.sum(chosen.astype(jnp.int32)).reshape(1), tiles

    lists = {farthest: listed((distance == FAR) == farthest) for farthest in (True, False)}
    float_shape = functools.partial(jax.ShapeDtypeStruct, dtype=jnp.float32)
    half = width_k // 2
    shapes = {
        True: float_shape((2, half, terms_here)),
        False: float_shape((col_count, width_k, terms_here)),
    }

    def first_product(farthest):
        return call(
            functools.partial(multiply_kernel, farthest),
            shapes[farthest],
            [SMEM] * 4 + [VMEM] + [ANY] * len(lines),
            [
                pltpu.VMEM((row_count, width_k, terms_here), jnp.bfloat16),
                pltpu.SemaphoreType.DMA((len(lines),)),
            ],
            flops=2**30 if farthest else 2**32,
        )(*lists[farthest], distance, line_slot(tile_cols), ppmi, *lines)

    def second_product(farthest, gathered):
        depth = 4
        return call(
            functools.partial(image_multiply_kernel, farthest),
            shapes[farthest],
            [SMEM] * 4 + [ANY, VMEM],
            [
                pltpu.VMEM((depth, width_k, terms_here), jnp.float32),
                pltpu.VMEM((2 * width_k, terms_here), jnp.bfloat16),
                pltpu.SemaphoreType.DMA((depth,)),
            ],
            mib=56,
            flops=2**30 if farthest else 2**32,
        )(*lists[farthest], distance, tile_cols, gathered, ppmi)

    block = pltpu.VMEM((TILE, TILE), jnp.float32)
    blocks = pltpu.VMEM((len(PAIRS), TILE, TILE), jnp.float32)

    def factor_step(j, *given):
        shape = [float_shape((BLOCKS - j, TILE, TILE))]
        if j + 1 < BLOCKS:
            shape.append(float_shape((len([pair for pair in PAIRS if pair[1] > j]), TILE, TILE)))
        return call(
            functools.partial(step_kernel, j),
            shape,
            [VMEM] if j else [SMEM, VMEM, VMEM],
            [block] if j else [block, blocks],
            flops=2**32,
        )(*given)

    def next_step(state):
        *cols, rest = state
        return [*cols, *factor_step(len(cols), rest)]

    solve = call(
        solve_kernel, float_shape((width_k, terms_here)), [SMEM] + [VMEM] * 3, [blocks, block]
    )
    gram_shape = float_shape((HALF, TILE, TILE))
    gram = call(gram_kernel, gram_shape, [SMEM, VMEM, VMEM])
    solve_gram = call(
        solve_gram_kernel,
        [float_shape((width_k, terms_here)), gram_shape],
        [SMEM] + [VMEM] * (BLOCKS + 2),
        [pltpu.VMEM((width_k, 2 * terms_here), jnp.float32)],
    )
    image, _ = ring_sum(first_product(True), first_product(False))
    gathered = lax.all_gather(image, ROWS, axis=0)
    own, other = gram_sum(gram(core, image, swap_core(image)))
    state = factor_step(0, core, own, other)
    gathered, state = lax.optimization_barrier((gathered, state))
    product, cols = ring_sum(
        second_product(True, gathered), second_product(False, gathered), [next_step] * (BLOCKS - 1), state
    )
    image, part = solve_gram(core, *cols, product, swap_core(product))
    return solve(core, *gram_sum(part), image)


def solution(mesh):
    rows, cols = mesh.shape["rows"], mesh.shape["cols"]
    side = 4
    devices = mesh.devices.reshape(side, rows // (2 * side), 2, cols)
    inner = Mesh(devices, ("x", "y", "core", "z"))
    lists = (*ROWS, "z")
    terms = ("z", *ROWS)
    in_specs = (P(None, terms), P(lists, None, None), P(lists), P(lists), P(lists), P())
    return jax.shard_map(
        local, mesh=inner, in_specs=in_specs, out_specs=P(None, terms), check_vma=False
    )
```

```python
import functools

import jax
import jax.numpy as jnp
from jax import lax
from jax.experimental import pallas as pl
from jax.experimental.pallas import tpu as pltpu
from jax.sharding import Mesh, PartitionSpec as P

HIGHEST = lax.Precision.HIGHEST
TILE = 128
SUB = 8
BLOCKS = 4
PAIRS = [(i, j) for i in range(BLOCKS) for j in range(i + 1)]
PLACE = {pair: n for n, pair in enumerate(PAIRS)}
HALF = len(PAIRS) // 2
FAR = 4
PART = 64
GROUP = 2
ROWS = ("x", "y", "core")
PLANE = ("x", "y")
VMEM = pl.BlockSpec(memory_space=pltpu.VMEM)
ANY = pl.BlockSpec(memory_space=pl.ANY)
SMEM = pl.BlockSpec(memory_space=pltpu.SMEM)


def dot_nt(a, b, precision=HIGHEST):
    return lax.dot_general(
        a, b, (((1,), (1,)), ((), ())), precision=precision, preferred_element_type=jnp.float32
    )


def dot_nn(a, b):
    return jnp.dot(a, b, precision=HIGHEST, preferred_element_type=jnp.float32)


def call(kernel, out_shape, in_specs, scratch=(), mib=16, flops=0):
    return pl.pallas_call(
        kernel,
        out_shape=out_shape,
        in_specs=in_specs,
        out_specs=jax.tree.map(lambda shape: VMEM, out_shape),
        scratch_shapes=list(scratch),
        compiler_params=pltpu.CompilerParams(vmem_limit_bytes=mib * 1024 * 1024),
        cost_estimate=pl.CostEstimate(flops=flops, bytes_accessed=2**22, transcendentals=0),
    )


def add_products(farthest, out_ref, rows, products):
    half = out_ref.shape[1]
    for distance, product in zip(rows, products):
        if farthest:
            product = jnp.where(distance == FAR, product, 0.0)
            for n in range(2):
                out_ref[n] = out_ref[n] + product[n * half : (n + 1) * half]
        else:
            out_ref[distance] = out_ref[distance] + product


def multiply_kernel(farthest, count_ref, tiles_ref, rows_ref, cols_ref, ppmi_ref, *refs):
    *pieces, out_ref, basis_ref, sems = refs
    size = pieces[0].shape[0]
    copies = [
        pltpu.make_async_copy(piece, basis_ref.at[pl.ds(n * size, size)], sems.at[n])
        for n, piece in enumerate(pieces)
    ]
    for copy in copies:
        copy.start()
    out_ref[...] = jnp.zeros_like(out_ref)
    for copy in copies:
        copy.wait()

    def add_tiles(group, carry):
        members = [group * GROUP + n for n in range(GROUP)]
        products = [dot_nt(basis_ref[cols_ref[n]], ppmi_ref[tiles_ref[n]], None) for n in members]
        add_products(farthest, out_ref, [rows_ref[n] for n in members], products)
        return carry

    lax.fori_loop(0, count_ref[0], add_tiles, 0)


def image_multiply_kernel(farthest, count_ref, tiles_ref, rows_ref, cols_ref, ppmi_ref, *refs):
    *pieces, out_ref, columns_ref, parts_ref, sems = refs
    count = count_ref[0] * GROUP
    depth = columns_ref.shape[0]
    width = columns_ref.shape[1]
    size = pieces[0].shape[0]

    def copy(piece, entry, n):
        slot = lax.rem(n, depth)
        return pltpu.make_async_copy(piece.at[entry], columns_ref.at[slot], sems.at[slot])

    def fetch(n):
        place = cols_ref[n]
        for k, piece in enumerate(pieces):

            @pl.when(place // size == k)
            def _():
                copy(piece, place % size, n).start()

    for n in range(depth - GROUP):

        @pl.when(n < count)
        def _():
            fetch(n)

    out_ref[...] = jnp.zeros_like(out_ref)

    def add_tiles(group, carry):
        members = [group * GROUP + n for n in range(GROUP)]
        for n in members:

            @pl.when(n + depth - GROUP < count)
            def _():
                fetch(n + depth - GROUP)

        products = []
        for n in members:
            copy(pieces[0], 0, n).wait()
        for k, n in enumerate(members):
            column = columns_ref[lax.rem(n, depth)]
            high = column.astype(jnp.bfloat16)
            parts_ref[k, pl.ds(0, width), :] = high
            parts_ref[k, pl.ds(width, width), :] = (column - high.astype(jnp.float32)).astype(jnp.bfloat16)
            product = dot_nt(parts_ref[k], ppmi_ref[tiles_ref[n]], None)
            products.append(product[:width] + product[width:])
        add_products(farthest, out_ref, [rows_ref[n] for n in members], products)
        return carry

    lax.fori_loop(0, count_ref[0], add_tiles, 0)


def gram_half(core, parts, out_ref):
    for n in range(HALF):
        first, second = PAIRS[n], PAIRS[HALF + n]
        i = pl.multiple_of(jnp.where(core == 0, first[0], second[0]) * TILE, TILE)
        j = pl.multiple_of(jnp.where(core == 0, first[1], second[1]) * TILE, TILE)
        out_ref[n] = sum(dot_nt(ref[pl.ds(i, TILE), :], ref[pl.ds(j, TILE), :]) for ref in parts)


def gram_kernel(core_ref, own_ref, other_ref, out_ref):
    gram_half(core_ref[0], [own_ref, other_ref], out_ref)


def spread_row(x, m):
    return jnp.broadcast_to(x[m : m + 1, :], (SUB, TILE))


def spread_col(x, lane):
    return jnp.broadcast_to(x[:, lane : lane + 1], (SUB, TILE))


def eliminate(a, base, keep, write):
    lane = lax.broadcasted_iota(jnp.int32, (SUB, TILE), 1)
    n = len(a)
    for p in range(n):
        first = base + SUB * p
        inside = (lane >= first) & (lane < first + SUB)
        cols = [[spread_col(a[i], first + k) for i in range(p, n)] for k in range(SUB)]
        s = [[spread_row(cols[k][0], q) if q >= k else None for k in range(SUB)] for q in range(SUB)]
        t = [
            jnp.where(inside, jnp.where(lane == first + k, 1.0, 0.0), spread_row(a[p], k))
            for k in range(SUB)
        ]
        following = [cols[k][1] for k in range(SUB)] if p + 1 < n else None
        low = [[None] * SUB for _ in range(SUB)]
        inverse = [None] * SUB
        for k in range(SUB):
            inverse[k] = pl.reciprocal(s[k][k], approx=True)
            for q in range(k + 1, SUB):
                low[q][k] = s[q][k] * inverse[k]
            for q in range(k + 1, SUB):
                for j in range(k + 1, q + 1):
                    if q == k + 1:
                        s[q][j] = s[q][j] - (s[q][k] * s[j][k]) * inverse[k]
                    else:
                        s[q][j] = s[q][j] - low[q][k] * s[j][k]
            for q in range(k + 1, SUB):
                t[q] = t[q] - low[q][k] * t[k]
                if following is not None:
                    following[q] = following[q] - low[q][k] * following[k]
        shown = (lane < first + SUB) | (lane >= keep)
        for k in range(SUB):
            write(first + k, jnp.where(shown, t[k] * lax.rsqrt(s[k][k]), 0.0))
        if following is None:
            break
        t = [t[k] * inverse[k] for k in range(SUB)]
        x = jnp.where(inside, 0.0, a[p + 1])
        for k in range(SUB):
            x = x - following[k] * t[k]
        a[p + 1] = x
        z = [None] * SUB
        for k in reversed(range(SUB)):
            x = t[k]
            for q in range(k + 1, SUB):
                x = x - low[q][k] * z[q]
            z[k] = x
        for i in range(p + 2, n):
            x = jnp.where(inside, 0.0, a[i])
            for k in range(SUB):
                x = x - cols[k][i - p] * z[k]
            a[i] = x


def factor_inverse(read, w_ref):
    a = [read(i) for i in range(TILE // SUB)]
    lane = lax.broadcasted_iota(jnp.int32, (PART, TILE), 1)

    def write(r, value):
        w_ref[pl.ds(r, 1), :] = value[0:1, :]

    step = PART // SUB
    eliminate(a[:step], 0, PART, write)
    top = w_ref[pl.ds(0, PART), :]
    w_ref[pl.ds(0, PART), :] = jnp.where(lane < PART, top, 0.0)
    change = lax.dot_general(
        top, top, (((0,), (0,)), ((), ())), precision=HIGHEST, preferred_element_type=jnp.float32
    )
    a = [
        jnp.where(lane[:SUB] < PART, 0.0, a[i]) - change[SUB * i : SUB * (i + 1), :]
        for i in range(step, TILE // SUB)
    ]
    eliminate(a, PART, TILE, write)


def factorize(core_ref, own_ref, other_ref, a_ref, w_ref, step):
    core = core_ref[0]
    for n in range(HALF):
        a_ref[core * HALF + n] = own_ref[n]
        a_ref[(1 - core) * HALF + n] = other_ref[n]
    factor = {}
    for j in range(BLOCKS):
        here = PLACE[j, j]

        def read(i):
            return a_ref[here, pl.ds(SUB * i, SUB), :]

        factor_inverse(read, w_ref)
        inverse = w_ref[...]
        for i in range(j + 1, BLOCKS):
            factor[i, j] = dot_nt(a_ref[PLACE[i, j]], inverse)
        for i in range(j + 1, BLOCKS):
            for k in range(j + 1, i + 1):
                n = PLACE[i, k]
                a_ref[n] = a_ref[n] - dot_nt(factor[i, j], factor[k, j])
        step(j, factor, inverse)


def solve_kernel(core_ref, own_ref, other_ref, image_ref, out_ref, a_ref, w_ref):
    solved = []

    def step(j, factor, inverse):
        rest = image_ref[pl.ds(TILE * j, TILE), :]
        for i in range(j):
            rest = rest - dot_nn(factor[j, i], solved[i])
        solved.append(dot_nn(inverse, rest))
        out_ref[pl.ds(TILE * j, TILE), :] = solved[j]

    factorize(core_ref, own_ref, other_ref, a_ref, w_ref, step)


def step_kernel(j, *refs):
    left = [pair for pair in PAIRS if pair[1] >= j]
    later = [pair for pair in PAIRS if pair[1] > j]
    rest_ref = None
    if j == 0:
        core_ref, own_ref, other_ref, col_ref, rest_ref, w_ref, a_ref = refs
        core = core_ref[0]
        for n in range(HALF):
            a_ref[core * HALF + n] = own_ref[n]
            a_ref[(1 - core) * HALF + n] = other_ref[n]
    elif later:
        a_ref, col_ref, rest_ref, w_ref = refs
    else:
        a_ref, col_ref, w_ref = refs

    def read(i):
        return a_ref[left.index((j, j)), pl.ds(SUB * i, SUB), :]

    factor_inverse(read, w_ref)
    inverse = w_ref[...]
    col_ref[0] = inverse
    factor = {i: dot_nt(a_ref[left.index((i, j))], inverse) for i in range(j + 1, BLOCKS)}
    for i in factor:
        col_ref[i - j] = factor[i]
    for n, (i, k) in enumerate(later):
        rest_ref[n] = a_ref[left.index((i, k))] - dot_nt(factor[i], factor[k])


def solve_gram_kernel(core_ref, *refs):
    *cols, own_ref, other_ref, image_ref, out_ref, solved_ref = refs
    width = own_ref.shape[1]
    solved = []
    for j in range(BLOCKS):
        here = pl.ds(TILE * j, TILE)
        rest = jnp.concatenate([own_ref[here, :], other_ref[here, :]], axis=1)
        for i in range(j):
            rest = rest - dot_nn(cols[i][j - i], solved[i])
        solved.append(dot_nn(cols[j][0], rest))
        solved_ref[here, :] = solved[j]
        image_ref[here, :] = solved[j][:, :width]
    gram_half(core_ref[0], [solved_ref], out_ref)


def swap_core(x):
    return lax.ppermute(x, "core", [(0, 1), (1, 0)])


def shift(x, step, turned):
    side_x, side_y = lax.axis_size("x"), lax.axis_size("y")
    pairs = []
    for i in range(side_x):
        for j in range(side_y):
            for core in range(2):
                to = (i + step) % side_x, j
                if turned != bool(core):
                    to = i, (j + step) % side_y
                pairs.append(((i * side_y + j) * 2 + core, (to[0] * side_y + to[1]) * 2 + core))
    return lax.ppermute(x, ROWS, pairs)


def gather_line(x):
    return [shift(x, step, False) for step in (1, 2, 3)]


def gather_plane(line):
    return [line] + [shift(line, step, True) for step in (1, 2, 3)]


def gather_cores(lines):
    return lines + [swap_core(line) for line in lines]


def line_slot(column):
    core = column % 2
    along_x = (lax.axis_index("x") - column // 8) % 4
    along_y = (lax.axis_index("y") - column // 2 % 4) % 4
    inside = jnp.where(core == 0, along_y * 4 + along_x, along_x * 4 + along_y)
    return inside + jnp.where(core == lax.axis_index("core"), 0, 16)


def ring_sum(far, parts, work=(), state=()):
    size = lax.axis_size("z")

    def up(x):
        return lax.ppermute(x, "z", [(i, (i + 1) % size) for i in range(size)])

    def down(x):
        return lax.ppermute(x, "z", [((i + 1) % size, i) for i in range(size)])

    half = far.shape[1]
    right = jnp.pad(up(far[0]), ((0, half), (0, 0)))
    left = jnp.pad(down(far[1]), ((half, 0), (0, 0)))
    for step in range(1, FAR):
        right, left, state = lax.optimization_barrier(
            (parts[FAR - step] + right, parts[FAR + step] + left, state)
        )
        right, left = up(right), down(left)
        if work:
            state = work[step - 1](state)
            right, left, state = lax.optimization_barrier((right, left, state))
    return parts[0] + right + left, state


def plane_sum(part):
    plane = lax.axis_size(PLANE)
    part = part.reshape(plane, HALF * TILE // plane, TILE)
    return jnp.sum(lax.all_to_all(part, PLANE, 0, 0), axis=0)


def depth_sum(part):
    part = jnp.broadcast_to(part[None], (lax.axis_size("z"),) + part.shape)
    return jnp.sum(lax.all_to_all(part, "z", 0, 0), axis=0)


def plane_gather(part):
    part = jnp.broadcast_to(part[None], (lax.axis_size(PLANE),) + part.shape)
    part = lax.all_to_all(part, PLANE, 0, 0).reshape(HALF, TILE, TILE)
    return part, swap_core(part)


def local(basis, tile_counts, tile_rows, tile_cols, tile_live, marginals):
    width_k, terms_here = basis.shape
    capacity, tile_size, _ = tile_counts.shape
    row_count = lax.axis_size(ROWS)
    col_count = lax.axis_size("z")
    row_index = lax.axis_index(ROWS)
    col_index = lax.axis_index("z")
    core = lax.axis_index("core").astype(jnp.int32).reshape(1)
    group_size = row_count * terms_here
    block = basis.astype(jnp.bfloat16)
    line = jnp.stack([block] + gather_line(block))
    line, marginals, tile_rows, tile_cols, tile_live = lax.optimization_barrier(
        (line, marginals, tile_rows, tile_cols, tile_live)
    )
    lines = gather_cores(gather_plane(line))
    marg_float = marginals.astype(jnp.float32)
    grand_total = jnp.sum(marg_float)
    log_margins = jnp.log(marg_float)
    row_logs = lax.dynamic_index_in_dim(
        log_margins.reshape(col_count, row_count, terms_here), row_index, 1, keepdims=False
    )
    col_logs = lax.dynamic_slice_in_dim(log_margins, col_index * group_size, group_size).reshape(
        -1, tile_size
    )
    log_ratio = (
        jnp.log(jnp.maximum(tile_counts.astype(jnp.float32), 1.0))
        + jnp.log(grand_total)
        - jnp.take(row_logs, tile_rows, axis=0)[:, :, None]
        - jnp.take(col_logs, tile_cols, axis=0)[:, None, :]
    )
    position = jnp.arange(capacity, dtype=jnp.int32)
    keep_mask = (tile_counts > 0) & (position < tile_live[0])[:, None, None]
    ppmi = jnp.where(keep_mask, jnp.maximum(log_ratio, 0.0), 0.0).astype(jnp.bfloat16)
    distance = (tile_rows - col_index) % col_count

    slots = line_slot(tile_cols)

    def listed(farthest):
        chosen = ((distance == FAR) == farthest) & (position < tile_live[0])
        rank = jnp.sum((chosen[None, :] & (position[None, :] < position[:, None])).astype(jnp.int32), axis=1)
        placed = chosen[:, None] & (rank[:, None] == position[None, :])

        def pick(values):
            return jnp.sum(jnp.where(placed, values[:, None], 0), axis=0)

        count = jnp.sum(chosen.astype(jnp.int32))
        rows = jnp.where(position < count, pick(distance), 0 if farthest else FAR)
        return ((count + GROUP - 1) // GROUP).reshape(1), pick(position), rows, pick(slots)

    lists = {farthest: listed(farthest) for farthest in (True, False)}
    float_shape = functools.partial(jax.ShapeDtypeStruct, dtype=jnp.float32)
    half = width_k // 2
    shapes = {
        True: float_shape((2, half, terms_here)),
        False: float_shape((col_count, width_k, terms_here)),
    }

    def first_product(farthest):
        return call(
            functools.partial(multiply_kernel, farthest),
            shapes[farthest],
            [SMEM] * 4 + [VMEM] + [ANY] * len(lines),
            [
                pltpu.VMEM((row_count, width_k, terms_here), jnp.bfloat16),
                pltpu.SemaphoreType.DMA((len(lines),)),
            ],
            flops=2**30 if farthest else 2**32,
        )(*lists[farthest], ppmi, *lines)

    def second_product(farthest, lines):
        depth = 4 * GROUP
        return call(
            functools.partial(image_multiply_kernel, farthest),
            shapes[farthest],
            [SMEM] * 4 + [VMEM] + [ANY] * len(lines),
            [
                pltpu.VMEM((depth, width_k, terms_here), jnp.float32),
                pltpu.VMEM((GROUP, 2 * width_k, terms_here), jnp.bfloat16),
                pltpu.SemaphoreType.DMA((depth,)),
            ],
            mib=32,
            flops=2**30 if farthest else 2**32,
        )(*lists[farthest], ppmi, *lines)

    square = pltpu.VMEM((TILE, TILE), jnp.float32)
    blocks = pltpu.VMEM((len(PAIRS), TILE, TILE), jnp.float32)

    def factor_step(j, *given):
        shape = [float_shape((BLOCKS - j, TILE, TILE))]
        if j + 1 < BLOCKS:
            shape.append(float_shape((len([pair for pair in PAIRS if pair[1] > j]), TILE, TILE)))
        return call(
            functools.partial(step_kernel, j),
            shape,
            [VMEM] if j else [SMEM, VMEM, VMEM],
            [square] if j else [square, blocks],
            flops=2**32,
        )(*given)

    def next_step(state):
        cols, rest = state
        col, *rest = factor_step(len(cols), *rest)
        return [*cols, col], rest

    solve = call(
        solve_kernel, float_shape((width_k, terms_here)), [SMEM] + [VMEM] * 3, [blocks, square]
    )
    gram_shape = float_shape((HALF, TILE, TILE))
    gram = call(gram_kernel, gram_shape, [SMEM, VMEM, VMEM])
    solve_gram = call(
        solve_gram_kernel,
        [float_shape((width_k, terms_here)), gram_shape],
        [SMEM] + [VMEM] * (BLOCKS + 2),
        [pltpu.VMEM((width_k, 2 * terms_here), jnp.float32)],
    )
    image, _ = ring_sum(first_product(True), first_product(False))
    near = gather_line(image)
    part = plane_sum(gram(core, image, swap_core(image)))
    near, part = lax.optimization_barrier((near, part))
    line, part = lax.optimization_barrier((jnp.stack([image] + near), part))
    lines, part = lax.optimization_barrier((gather_plane(line), depth_sum(part)))
    lines = gather_cores(lines)
    own, other = plane_gather(part)
    work = [next_step, next_step, lambda state: next_step(next_step(state))]
    state = ([], [core, own, other])
    product, (cols, _) = ring_sum(second_product(True, lines), second_product(False, lines), work, state)
    image, part = solve_gram(core, *cols, product, swap_core(product))
    return solve(core, *plane_gather(depth_sum(plane_sum(part))), image)


def solution(mesh):
    rows, cols = mesh.shape["rows"], mesh.shape["cols"]
    side = 4
    devices = mesh.devices.reshape(side, rows // (2 * side), 2, cols)
    inner = Mesh(devices, ("x", "y", "core", "z"))
    lists = (*ROWS, "z")
    terms = ("z", *ROWS)
    in_specs = (P(None, terms), P(lists, None, None), P(lists), P(lists), P(lists), P())
    return jax.shard_map(
        local, mesh=inner, in_specs=in_specs, out_specs=P(None, terms), check_vma=False
    )
```

```python
import functools

import jax
import jax.numpy as jnp
from jax import lax
from jax.experimental import pallas as pl
from jax.experimental.pallas import tpu as pltpu
from jax.sharding import Mesh, PartitionSpec as P

HIGHEST = lax.Precision.HIGHEST
TILE = 128
SUB = 8
BLOCKS = 4
PAIRS = [(i, j) for i in range(BLOCKS) for j in range(i + 1)]
PLACE = {pair: n for n, pair in enumerate(PAIRS)}
HALF = len(PAIRS) // 2
FAR = 4
PART = 64
GROUP = 2
ROWS = ("x", "y", "core")
PLANE = ("x", "y")
VMEM = pl.BlockSpec(memory_space=pltpu.VMEM)
ANY = pl.BlockSpec(memory_space=pl.ANY)
SMEM = pl.BlockSpec(memory_space=pltpu.SMEM)


def dot_nt(a, b, precision=HIGHEST):
    return lax.dot_general(
        a, b, (((1,), (1,)), ((), ())), precision=precision, preferred_element_type=jnp.float32
    )


def dot_nn(a, b):
    return jnp.dot(a, b, precision=HIGHEST, preferred_element_type=jnp.float32)


def call(kernel, out_shape, in_specs, scratch=(), mib=16, flops=0):
    return pl.pallas_call(
        kernel,
        out_shape=out_shape,
        in_specs=in_specs,
        out_specs=jax.tree.map(lambda shape: VMEM, out_shape),
        scratch_shapes=list(scratch),
        compiler_params=pltpu.CompilerParams(vmem_limit_bytes=mib * 1024 * 1024),
        cost_estimate=pl.CostEstimate(flops=flops, bytes_accessed=2**22, transcendentals=0),
    )


def add_products(farthest, out_ref, rows, products):
    half = out_ref.shape[1]
    for distance, product in zip(rows, products):
        if farthest:
            product = jnp.where(distance == FAR, product, 0.0)
            for n in range(2):
                out_ref[n] = out_ref[n] + product[n * half : (n + 1) * half]
        else:
            out_ref[distance] = out_ref[distance] + product


def multiply_kernel(farthest, count_ref, tiles_ref, rows_ref, cols_ref, ppmi_ref, *refs):
    *pieces, out_ref, basis_ref, sems = refs
    size = pieces[0].shape[0]
    copies = [
        pltpu.make_async_copy(piece, basis_ref.at[pl.ds(n * size, size)], sems.at[n])
        for n, piece in enumerate(pieces)
    ]
    for copy in copies:
        copy.start()
    out_ref[...] = jnp.zeros_like(out_ref)
    for copy in copies:
        copy.wait()

    def add_tiles(group, carry):
        members = [group * GROUP + n for n in range(GROUP)]
        products = [dot_nt(basis_ref[cols_ref[n]], ppmi_ref[tiles_ref[n]], None) for n in members]
        add_products(farthest, out_ref, [rows_ref[n] for n in members], products)
        return carry

    lax.fori_loop(0, count_ref[0], add_tiles, 0)


def image_multiply_kernel(farthest, count_ref, tiles_ref, rows_ref, cols_ref, ppmi_ref, *refs):
    *pieces, out_ref, columns_ref, parts_ref, sems = refs
    count = count_ref[0] * GROUP
    depth = columns_ref.shape[0]
    width = columns_ref.shape[1]
    size = pieces[0].shape[0]

    def copy(piece, entry, n):
        slot = lax.rem(n, depth)
        return pltpu.make_async_copy(piece.at[entry], columns_ref.at[slot], sems.at[slot])

    def fetch(n):
        place = cols_ref[n]
        for k, piece in enumerate(pieces):

            @pl.when(place // size == k)
            def _():
                copy(piece, place % size, n).start()

    for n in range(depth - GROUP):

        @pl.when(n < count)
        def _():
            fetch(n)

    out_ref[...] = jnp.zeros_like(out_ref)

    def add_tiles(group, carry):
        members = [group * GROUP + n for n in range(GROUP)]
        for n in members:

            @pl.when(n + depth - GROUP < count)
            def _():
                fetch(n + depth - GROUP)

        products = []
        for n in members:
            copy(pieces[0], 0, n).wait()
        for k, n in enumerate(members):
            column = columns_ref[lax.rem(n, depth)]
            high = column.astype(jnp.bfloat16)
            parts_ref[k, pl.ds(0, width), :] = high
            parts_ref[k, pl.ds(width, width), :] = (column - high.astype(jnp.float32)).astype(jnp.bfloat16)
            product = dot_nt(parts_ref[k], ppmi_ref[tiles_ref[n]], None)
            products.append(product[:width] + product[width:])
        add_products(farthest, out_ref, [rows_ref[n] for n in members], products)
        return carry

    lax.fori_loop(0, count_ref[0], add_tiles, 0)


def gram_half(core, parts, out_ref):
    for n in range(HALF):
        first, second = PAIRS[n], PAIRS[HALF + n]
        i = pl.multiple_of(jnp.where(core == 0, first[0], second[0]) * TILE, TILE)
        j = pl.multiple_of(jnp.where(core == 0, first[1], second[1]) * TILE, TILE)
        out_ref[n] = sum(dot_nt(ref[pl.ds(i, TILE), :], ref[pl.ds(j, TILE), :]) for ref in parts)


def gram_kernel(core_ref, own_ref, other_ref, out_ref):
    gram_half(core_ref[0], [own_ref, other_ref], out_ref)


def spread_row(x, m):
    return jnp.broadcast_to(x[m : m + 1, :], (SUB, TILE))


def spread_col(x, lane):
    return jnp.broadcast_to(x[:, lane : lane + 1], (SUB, TILE))


def eliminate(a, base, keep, write, c_ref):
    lane = lax.broadcasted_iota(jnp.int32, (SUB, TILE), 1)
    n = len(a)
    for p in range(n):
        first = base + SUB * p
        inside = (lane >= first) & (lane < first + SUB)
        cols = [[spread_col(a[i], first + k) for i in range(p, n)] for k in range(SUB)]
        place = PART * (p % 2)
        for k in range(SUB):
            c_ref[pl.ds(place + SUB * k, SUB), :] = cols[k][0]
        s = [[None] * SUB for _ in range(SUB)]
        for q in range(SUB):
            for k in range(q + 1):
                s[q][k] = jnp.broadcast_to(c_ref[pl.ds(place + SUB * k + q, 1), :], (SUB, TILE))
        t = [
            jnp.where(inside, jnp.where(lane == first + k, 1.0, 0.0), spread_row(a[p], k))
            for k in range(SUB)
        ]
        following = [cols[k][1] for k in range(SUB)] if p + 1 < n else None
        low = [[None] * SUB for _ in range(SUB)]
        inverse = [None] * SUB
        for k in range(SUB):
            inverse[k] = pl.reciprocal(s[k][k], approx=True)
            for q in range(k + 1, SUB):
                low[q][k] = s[q][k] * inverse[k]
            for q in range(k + 1, SUB):
                for j in range(k + 1, q + 1):
                    if q == k + 1:
                        s[q][j] = s[q][j] - (s[q][k] * s[j][k]) * inverse[k]
                    else:
                        s[q][j] = s[q][j] - low[q][k] * s[j][k]
            for q in range(k + 1, SUB):
                t[q] = t[q] - low[q][k] * t[k]
                if following is not None:
                    following[q] = following[q] - low[q][k] * following[k]
        shown = (lane < first + SUB) | (lane >= keep)
        for k in range(SUB):
            write(first + k, jnp.where(shown, t[k] * lax.rsqrt(s[k][k]), 0.0))
        if following is None:
            break
        t = [t[k] * inverse[k] for k in range(SUB)]
        x = jnp.where(inside, 0.0, a[p + 1])
        for k in range(SUB):
            x = x - following[k] * t[k]
        a[p + 1] = x
        z = [None] * SUB
        for k in reversed(range(SUB)):
            x = t[k]
            for q in range(k + 1, SUB):
                x = x - low[q][k] * z[q]
            z[k] = x
        for i in range(p + 2, n):
            x = jnp.where(inside, 0.0, a[i])
            for k in range(SUB):
                x = x - cols[k][i - p] * z[k]
            a[i] = x


def factor_inverse(read, w_ref, c_ref):
    a = [read(i) for i in range(TILE // SUB)]
    lane = lax.broadcasted_iota(jnp.int32, (PART, TILE), 1)

    def write(r, value):
        w_ref[pl.ds(r, 1), :] = value[0:1, :]

    step = PART // SUB
    eliminate(a[:step], 0, PART, write, c_ref)
    top = w_ref[pl.ds(0, PART), :]
    w_ref[pl.ds(0, PART), :] = jnp.where(lane < PART, top, 0.0)
    change = lax.dot_general(
        top, top, (((0,), (0,)), ((), ())), precision=HIGHEST, preferred_element_type=jnp.float32
    )
    a = [
        jnp.where(lane[:SUB] < PART, 0.0, a[i]) - change[SUB * i : SUB * (i + 1), :]
        for i in range(step, TILE // SUB)
    ]
    eliminate(a, PART, TILE, write, c_ref)


def factorize(core_ref, own_ref, other_ref, a_ref, w_ref, c_ref, step):
    core = core_ref[0]
    for n in range(HALF):
        a_ref[core * HALF + n] = own_ref[n]
        a_ref[(1 - core) * HALF + n] = other_ref[n]
    factor = {}
    for j in range(BLOCKS):
        here = PLACE[j, j]

        def read(i):
            return a_ref[here, pl.ds(SUB * i, SUB), :]

        factor_inverse(read, w_ref, c_ref)
        inverse = w_ref[...]
        for i in range(j + 1, BLOCKS):
            factor[i, j] = dot_nt(a_ref[PLACE[i, j]], inverse)
        for i in range(j + 1, BLOCKS):
            for k in range(j + 1, i + 1):
                n = PLACE[i, k]
                a_ref[n] = a_ref[n] - dot_nt(factor[i, j], factor[k, j])
        step(j, factor, inverse)


def solve_kernel(core_ref, own_ref, other_ref, image_ref, out_ref, a_ref, w_ref, c_ref):
    solved = []

    def step(j, factor, inverse):
        rest = image_ref[pl.ds(TILE * j, TILE), :]
        for i in range(j):
            rest = rest - dot_nn(factor[j, i], solved[i])
        solved.append(dot_nn(inverse, rest))
        out_ref[pl.ds(TILE * j, TILE), :] = solved[j]

    factorize(core_ref, own_ref, other_ref, a_ref, w_ref, c_ref, step)


def step_kernel(j, *refs):
    left = [pair for pair in PAIRS if pair[1] >= j]
    later = [pair for pair in PAIRS if pair[1] > j]
    rest_ref = None
    if j == 0:
        core_ref, own_ref, other_ref, col_ref, rest_ref, w_ref, c_ref, a_ref = refs
        core = core_ref[0]
        for n in range(HALF):
            a_ref[core * HALF + n] = own_ref[n]
            a_ref[(1 - core) * HALF + n] = other_ref[n]
    elif later:
        a_ref, col_ref, rest_ref, w_ref, c_ref = refs
    else:
        a_ref, col_ref, w_ref, c_ref = refs

    def read(i):
        return a_ref[left.index((j, j)), pl.ds(SUB * i, SUB), :]

    factor_inverse(read, w_ref, c_ref)
    inverse = w_ref[...]
    col_ref[0] = inverse
    factor = {i: dot_nt(a_ref[left.index((i, j))], inverse) for i in range(j + 1, BLOCKS)}
    for i in factor:
        col_ref[i - j] = factor[i]
    for n, (i, k) in enumerate(later):
        rest_ref[n] = a_ref[left.index((i, k))] - dot_nt(factor[i], factor[k])


def solve_gram_kernel(core_ref, *refs):
    *cols, own_ref, other_ref, image_ref, out_ref, solved_ref = refs
    width = own_ref.shape[1]
    solved = []
    for j in range(BLOCKS):
        here = pl.ds(TILE * j, TILE)
        rest = jnp.concatenate([own_ref[here, :], other_ref[here, :]], axis=1)
        for i in range(j):
            rest = rest - dot_nn(cols[i][j - i], solved[i])
        solved.append(dot_nn(cols[j][0], rest))
        solved_ref[here, :] = solved[j]
        image_ref[here, :] = solved[j][:, :width]
    gram_half(core_ref[0], [solved_ref], out_ref)


def swap_core(x):
    return lax.ppermute(x, "core", [(0, 1), (1, 0)])


def shift(x, step, turned):
    side_x, side_y = lax.axis_size("x"), lax.axis_size("y")
    pairs = []
    for i in range(side_x):
        for j in range(side_y):
            for core in range(2):
                to = (i + step) % side_x, j
                if turned != bool(core):
                    to = i, (j + step) % side_y
                pairs.append(((i * side_y + j) * 2 + core, (to[0] * side_y + to[1]) * 2 + core))
    return lax.ppermute(x, ROWS, pairs)


def gather_line(x):
    return [shift(x, step, False) for step in (1, 2, 3)]


def gather_plane(line):
    return [line] + [shift(line, step, True) for step in (1, 2, 3)]


def gather_cores(lines, beside):
    first = swap_core(lines[0])
    rest, beside = lax.optimization_barrier((lines[1:], beside))
    return [lines[0], *rest, first, *map(swap_core, rest)], beside


def line_slot(column):
    core = column % 2
    along_x = (lax.axis_index("x") - column // 8) % 4
    along_y = (lax.axis_index("y") - column // 2 % 4) % 4
    inside = jnp.where(core == 0, along_y * 4 + along_x, along_x * 4 + along_y)
    return inside + jnp.where(core == lax.axis_index("core"), 0, 16)


def ring_sum(far, parts, work=(), state=()):
    size = lax.axis_size("z")

    def up(x):
        return lax.ppermute(x, "z", [(i, (i + 1) % size) for i in range(size)])

    def down(x):
        return lax.ppermute(x, "z", [((i + 1) % size, i) for i in range(size)])

    half = far.shape[1]
    right = jnp.pad(up(far[0]), ((0, half), (0, 0)))
    left = jnp.pad(down(far[1]), ((half, 0), (0, 0)))
    for step in range(1, FAR):
        right, left, state = lax.optimization_barrier(
            (parts[FAR - step] + right, parts[FAR + step] + left, state)
        )
        right, left = up(right), down(left)
        if work:
            state = work[step - 1](state)
            right, left, state = lax.optimization_barrier((right, left, state))
    return parts[0] + right + left, state


def plane_sum(part):
    plane = lax.axis_size(PLANE)
    part = part.reshape(plane, HALF * TILE // plane, TILE)
    return jnp.sum(lax.all_to_all(part, PLANE, 0, 0), axis=0)


def depth_sum(part):
    part = jnp.broadcast_to(part[None], (lax.axis_size("z"),) + part.shape)
    return jnp.sum(lax.all_to_all(part, "z", 0, 0), axis=0)


def plane_gather(part):
    part = jnp.broadcast_to(part[None], (lax.axis_size(PLANE),) + part.shape)
    part = lax.all_to_all(part, PLANE, 0, 0).reshape(HALF, TILE, TILE)
    return part, swap_core(part)


def local(basis, tile_counts, tile_rows, tile_cols, tile_live, marginals):
    width_k, terms_here = basis.shape
    capacity, tile_size, _ = tile_counts.shape
    row_count = lax.axis_size(ROWS)
    col_count = lax.axis_size("z")
    row_index = lax.axis_index(ROWS)
    col_index = lax.axis_index("z")
    core = lax.axis_index("core").astype(jnp.int32).reshape(1)
    group_size = row_count * terms_here
    block = basis.astype(jnp.bfloat16)
    line = jnp.stack([block] + gather_line(block))
    line, marginals, tile_rows, tile_cols, tile_live = lax.optimization_barrier(
        (line, marginals, tile_rows, tile_cols, tile_live)
    )
    lines = gather_plane(line)
    marg_float = marginals.astype(jnp.float32)
    grand_total = jnp.sum(marg_float)
    log_margins = jnp.log(marg_float)
    row_logs = lax.dynamic_index_in_dim(
        log_margins.reshape(col_count, row_count, terms_here), row_index, 1, keepdims=False
    )
    col_logs = lax.dynamic_slice_in_dim(log_margins, col_index * group_size, group_size).reshape(
        -1, tile_size
    )
    log_ratio = (
        jnp.log(jnp.maximum(tile_counts.astype(jnp.float32), 1.0))
        + jnp.log(grand_total)
        - jnp.take(row_logs, tile_rows, axis=0)[:, :, None]
        - jnp.take(col_logs, tile_cols, axis=0)[:, None, :]
    )
    position = jnp.arange(capacity, dtype=jnp.int32)
    keep_mask = (tile_counts > 0) & (position < tile_live[0])[:, None, None]
    ppmi = jnp.where(keep_mask, jnp.maximum(log_ratio, 0.0), 0.0).astype(jnp.bfloat16)
    lines, ppmi = gather_cores(lines, ppmi)
    distance = (tile_rows - col_index) % col_count

    slots = line_slot(tile_cols)

    def listed(farthest):
        chosen = ((distance == FAR) == farthest) & (position < tile_live[0])
        rank = jnp.sum((chosen[None, :] & (position[None, :] < position[:, None])).astype(jnp.int32), axis=1)
        placed = chosen[:, None] & (rank[:, None] == position[None, :])

        def pick(values):
            return jnp.sum(jnp.where(placed, values[:, None], 0), axis=0)

        count = jnp.sum(chosen.astype(jnp.int32))
        rows = jnp.where(position < count, pick(distance), 0 if farthest else FAR)
        return ((count + GROUP - 1) // GROUP).reshape(1), pick(position), rows, pick(slots)

    lists = {farthest: listed(farthest) for farthest in (True, False)}
    float_shape = functools.partial(jax.ShapeDtypeStruct, dtype=jnp.float32)
    half = width_k // 2
    shapes = {
        True: float_shape((2, half, terms_here)),
        False: float_shape((col_count, width_k, terms_here)),
    }

    def first_product(farthest):
        return call(
            functools.partial(multiply_kernel, farthest),
            shapes[farthest],
            [SMEM] * 4 + [VMEM] + [ANY] * len(lines),
            [
                pltpu.VMEM((row_count, width_k, terms_here), jnp.bfloat16),
                pltpu.SemaphoreType.DMA((len(lines),)),
            ],
            flops=2**30 if farthest else 2**32,
        )(*lists[farthest], ppmi, *lines)

    def second_product(farthest, lines):
        depth = 4 * GROUP
        return call(
            functools.partial(image_multiply_kernel, farthest),
            shapes[farthest],
            [SMEM] * 4 + [VMEM] + [ANY] * len(lines),
            [
                pltpu.VMEM((depth, width_k, terms_here), jnp.float32),
                pltpu.VMEM((GROUP, 2 * width_k, terms_here), jnp.bfloat16),
                pltpu.SemaphoreType.DMA((depth,)),
            ],
            mib=32,
            flops=2**30 if farthest else 2**32,
        )(*lists[farthest], ppmi, *lines)

    square = pltpu.VMEM((TILE, TILE), jnp.float32)
    blocks = pltpu.VMEM((len(PAIRS), TILE, TILE), jnp.float32)

    def factor_step(j, *given):
        shape = [float_shape((BLOCKS - j, TILE, TILE))]
        if j + 1 < BLOCKS:
            shape.append(float_shape((len([pair for pair in PAIRS if pair[1] > j]), TILE, TILE)))
        return call(
            functools.partial(step_kernel, j),
            shape,
            [VMEM] if j else [SMEM, VMEM, VMEM],
            [square, square] if j else [square, square, blocks],
            flops=2**32,
        )(*given)

    def next_step(state):
        cols, rest = state
        col, *rest = factor_step(len(cols), *rest)
        return [*cols, col], rest

    solve = call(
        solve_kernel, float_shape((width_k, terms_here)), [SMEM] + [VMEM] * 3, [blocks, square, square]
    )
    gram_shape = float_shape((HALF, TILE, TILE))
    gram = call(gram_kernel, gram_shape, [SMEM, VMEM, VMEM])
    solve_gram = call(
        solve_gram_kernel,
        [float_shape((width_k, terms_here)), gram_shape],
        [SMEM] + [VMEM] * (BLOCKS + 2),
        [pltpu.VMEM((width_k, 2 * terms_here), jnp.float32)],
    )
    image, _ = ring_sum(first_product(True), first_product(False))
    near = gather_line(image)
    part = gram(core, image, swap_core(image))
    near, part = lax.optimization_barrier((near, part))
    near, part = lax.optimization_barrier((near, plane_sum(part)))
    line, part = lax.optimization_barrier((jnp.stack([image] + near), part))
    lines, part = gather_cores(gather_plane(line), depth_sum(part))
    own, other = plane_gather(part)
    work = [next_step, next_step, lambda state: next_step(next_step(state))]
    state = ([], [core, own, other])
    product, (cols, _) = ring_sum(second_product(True, lines), second_product(False, lines), work, state)
    image, part = solve_gram(core, *cols, product, swap_core(product))
    return solve(core, *plane_gather(depth_sum(plane_sum(part))), image)


def solution(mesh):
    rows, cols = mesh.shape["rows"], mesh.shape["cols"]
    side = 4
    devices = mesh.devices.reshape(side, rows // (2 * side), 2, cols)
    inner = Mesh(devices, ("x", "y", "core", "z"))
    lists = (*ROWS, "z")
    terms = ("z", *ROWS)
    in_specs = (P(None, terms), P(lists, None, None), P(lists), P(lists), P(lists), P())
    return jax.shard_map(
        local, mesh=inner, in_specs=in_specs, out_specs=P(None, terms), check_vma=False
    )
```

```python
import functools

import jax
import jax.numpy as jnp
from jax import lax
from jax.experimental import pallas as pl
from jax.experimental.pallas import tpu as pltpu
from jax.sharding import Mesh, PartitionSpec as P

HIGHEST = lax.Precision.HIGHEST
TILE = 128
SUB = 8
BLOCKS = 4
PAIRS = [(i, j) for i in range(BLOCKS) for j in range(i + 1)]
PLACE = {pair: n for n, pair in enumerate(PAIRS)}
HALF = len(PAIRS) // 2
FAR = 4
PART = 64
GROUP = 2
ROWS = ("x", "y", "core")
PLANE = ("x", "y")
VMEM = pl.BlockSpec(memory_space=pltpu.VMEM)
ANY = pl.BlockSpec(memory_space=pl.ANY)
SMEM = pl.BlockSpec(memory_space=pltpu.SMEM)


def dot_nt(a, b, precision=HIGHEST):
    return lax.dot_general(
        a, b, (((1,), (1,)), ((), ())), precision=precision, preferred_element_type=jnp.float32
    )


def dot_nn(a, b):
    return jnp.dot(a, b, precision=HIGHEST, preferred_element_type=jnp.float32)


def call(kernel, out_shape, in_specs, scratch=(), mib=16, flops=0):
    return pl.pallas_call(
        kernel,
        out_shape=out_shape,
        in_specs=in_specs,
        out_specs=jax.tree.map(lambda shape: VMEM, out_shape),
        scratch_shapes=list(scratch),
        compiler_params=pltpu.CompilerParams(vmem_limit_bytes=mib * 1024 * 1024),
        cost_estimate=pl.CostEstimate(flops=flops, bytes_accessed=2**22, transcendentals=0),
    )


def add_products(farthest, out_ref, rows, products):
    half = out_ref.shape[1]
    for distance, product in zip(rows, products):
        if farthest:
            product = jnp.where(distance == FAR, product, 0.0)
            for n in range(2):
                out_ref[n] = out_ref[n] + product[n * half : (n + 1) * half]
        else:
            out_ref[distance] = out_ref[distance] + product


def multiply_kernel(farthest, count_ref, tiles_ref, rows_ref, cols_ref, ppmi_ref, *refs):
    *pieces, out_ref, basis_ref, sems = refs
    size = pieces[0].shape[0]
    copies = [
        pltpu.make_async_copy(piece, basis_ref.at[pl.ds(n * size, size)], sems.at[n])
        for n, piece in enumerate(pieces)
    ]
    for copy in copies:
        copy.start()
    out_ref[...] = jnp.zeros_like(out_ref)
    for copy in copies:
        copy.wait()

    def add_tiles(group, carry):
        members = [group * GROUP + n for n in range(GROUP)]
        products = [dot_nt(basis_ref[cols_ref[n]], ppmi_ref[tiles_ref[n]], None) for n in members]
        add_products(farthest, out_ref, [rows_ref[n] for n in members], products)
        return carry

    lax.fori_loop(0, count_ref[0], add_tiles, 0)


def image_multiply_kernel(farthest, count_ref, tiles_ref, rows_ref, cols_ref, ppmi_ref, *refs):
    *pieces, out_ref, columns_ref, parts_ref, sems = refs
    count = count_ref[0] * GROUP
    depth = columns_ref.shape[0]
    width = columns_ref.shape[1]
    size = pieces[0].shape[0]

    def copy(piece, entry, n):
        slot = lax.rem(n, depth)
        return pltpu.make_async_copy(piece.at[entry], columns_ref.at[slot], sems.at[slot])

    def fetch(n):
        place = cols_ref[n]
        for k, piece in enumerate(pieces):

            @pl.when(place // size == k)
            def _():
                copy(piece, place % size, n).start()

    for n in range(depth - GROUP):

        @pl.when(n < count)
        def _():
            fetch(n)

    out_ref[...] = jnp.zeros_like(out_ref)

    def add_tiles(group, carry):
        members = [group * GROUP + n for n in range(GROUP)]
        for n in members:

            @pl.when(n + depth - GROUP < count)
            def _():
                fetch(n + depth - GROUP)

        products = []
        for n in members:
            copy(pieces[0], 0, n).wait()
        for k, n in enumerate(members):
            column = columns_ref[lax.rem(n, depth)]
            high = column.astype(jnp.bfloat16)
            parts_ref[k, pl.ds(0, width), :] = high
            parts_ref[k, pl.ds(width, width), :] = (column - high.astype(jnp.float32)).astype(jnp.bfloat16)
            product = dot_nt(parts_ref[k], ppmi_ref[tiles_ref[n]], None)
            products.append(product[:width] + product[width:])
        add_products(farthest, out_ref, [rows_ref[n] for n in members], products)
        return carry

    lax.fori_loop(0, count_ref[0], add_tiles, 0)


def gram_half(core, parts, out_ref):
    for n in range(HALF):
        first, second = PAIRS[n], PAIRS[HALF + n]
        i = pl.multiple_of(jnp.where(core == 0, first[0], second[0]) * TILE, TILE)
        j = pl.multiple_of(jnp.where(core == 0, first[1], second[1]) * TILE, TILE)
        out_ref[n] = sum(dot_nt(ref[pl.ds(i, TILE), :], ref[pl.ds(j, TILE), :]) for ref in parts)


def gram_kernel(core_ref, own_ref, other_ref, out_ref):
    gram_half(core_ref[0], [own_ref, other_ref], out_ref)


def spread_row(x, m):
    return jnp.broadcast_to(x[m : m + 1, :], (SUB, TILE))


def spread_col(x, lane):
    return jnp.broadcast_to(x[:, lane : lane + 1], (SUB, TILE))


def eliminate(a, base, keep, write, c_ref):
    lane = lax.broadcasted_iota(jnp.int32, (SUB, TILE), 1)
    n = len(a)
    for p in range(n):
        first = base + SUB * p
        inside = (lane >= first) & (lane < first + SUB)
        cols = [[spread_col(a[i], first + k) for i in range(p, n)] for k in range(SUB)]
        place = PART * (p % 2)
        for k in range(SUB):
            c_ref[pl.ds(place + SUB * k, SUB), :] = cols[k][0]
        s = [[None] * SUB for _ in range(SUB)]
        for q in range(SUB):
            for k in range(q + 1):
                s[q][k] = jnp.broadcast_to(c_ref[pl.ds(place + SUB * k + q, 1), :], (SUB, TILE))
        t = [
            jnp.where(inside, jnp.where(lane == first + k, 1.0, 0.0), spread_row(a[p], k))
            for k in range(SUB)
        ]
        following = [cols[k][1] for k in range(SUB)] if p + 1 < n else None
        low = [[None] * SUB for _ in range(SUB)]
        inverse = [None] * SUB
        for k in range(SUB):
            inverse[k] = pl.reciprocal(s[k][k], approx=True)
            for q in range(k + 1, SUB):
                low[q][k] = s[q][k] * inverse[k]
            for q in range(k + 1, SUB):
                for j in range(k + 1, q + 1):
                    if q == k + 1:
                        s[q][j] = s[q][j] - (s[q][k] * s[j][k]) * inverse[k]
                    else:
                        s[q][j] = s[q][j] - low[q][k] * s[j][k]
            for q in range(k + 1, SUB):
                t[q] = t[q] - low[q][k] * t[k]
                if following is not None:
                    following[q] = following[q] - low[q][k] * following[k]
        shown = (lane < first + SUB) | (lane >= keep)
        for k in range(SUB):
            write(first + k, jnp.where(shown, t[k] * lax.rsqrt(s[k][k]), 0.0))
        if following is None:
            break
        t = [t[k] * inverse[k] for k in range(SUB)]
        x = jnp.where(inside, 0.0, a[p + 1])
        for k in range(SUB):
            x = x - following[k] * t[k]
        a[p + 1] = x
        z = [None] * SUB
        for k in reversed(range(SUB)):
            x = t[k]
            for q in range(k + 1, SUB):
                x = x - low[q][k] * z[q]
            z[k] = x
        for i in range(p + 2, n):
            x = jnp.where(inside, 0.0, a[i])
            for k in range(SUB):
                x = x - cols[k][i - p] * z[k]
            a[i] = x


def factor_inverse(read, w_ref, c_ref):
    a = [read(i) for i in range(TILE // SUB)]
    lane = lax.broadcasted_iota(jnp.int32, (PART, TILE), 1)

    def write(r, value):
        w_ref[pl.ds(r, 1), :] = value[0:1, :]

    step = PART // SUB
    eliminate(a[:step], 0, PART, write, c_ref)
    top = w_ref[pl.ds(0, PART), :]
    w_ref[pl.ds(0, PART), :] = jnp.where(lane < PART, top, 0.0)
    change = lax.dot_general(
        top, top, (((0,), (0,)), ((), ())), precision=HIGHEST, preferred_element_type=jnp.float32
    )
    a = [
        jnp.where(lane[:SUB] < PART, 0.0, a[i]) - change[SUB * i : SUB * (i + 1), :]
        for i in range(step, TILE // SUB)
    ]
    eliminate(a, PART, TILE, write, c_ref)


def factorize(core_ref, own_ref, other_ref, a_ref, w_ref, c_ref, step):
    core = core_ref[0]
    for n in range(HALF):
        a_ref[core * HALF + n] = own_ref[n]
        a_ref[(1 - core) * HALF + n] = other_ref[n]
    factor = {}
    for j in range(BLOCKS):
        here = PLACE[j, j]

        def read(i):
            return a_ref[here, pl.ds(SUB * i, SUB), :]

        factor_inverse(read, w_ref, c_ref)
        inverse = w_ref[...]
        for i in range(j + 1, BLOCKS):
            factor[i, j] = dot_nt(a_ref[PLACE[i, j]], inverse)
        for i in range(j + 1, BLOCKS):
            for k in range(j + 1, i + 1):
                n = PLACE[i, k]
                a_ref[n] = a_ref[n] - dot_nt(factor[i, j], factor[k, j])
        step(j, factor, inverse)


def solve_kernel(core_ref, own_ref, other_ref, image_ref, out_ref, a_ref, w_ref, c_ref):
    solved = []

    def step(j, factor, inverse):
        rest = image_ref[pl.ds(TILE * j, TILE), :]
        for i in range(j):
            rest = rest - dot_nn(factor[j, i], solved[i])
        solved.append(dot_nn(inverse, rest))
        out_ref[pl.ds(TILE * j, TILE), :] = solved[j]

    factorize(core_ref, own_ref, other_ref, a_ref, w_ref, c_ref, step)


def step_kernel(j, *refs):
    left = [pair for pair in PAIRS if pair[1] >= j]
    later = [pair for pair in PAIRS if pair[1] > j]
    rest_ref = None
    if j == 0:
        core_ref, own_ref, other_ref, col_ref, rest_ref, w_ref, c_ref, a_ref = refs
        core = core_ref[0]
        for n in range(HALF):
            a_ref[core * HALF + n] = own_ref[n]
            a_ref[(1 - core) * HALF + n] = other_ref[n]
    elif later:
        a_ref, col_ref, rest_ref, w_ref, c_ref = refs
    else:
        a_ref, col_ref, w_ref, c_ref = refs

    def read(i):
        return a_ref[left.index((j, j)), pl.ds(SUB * i, SUB), :]

    factor_inverse(read, w_ref, c_ref)
    inverse = w_ref[...]
    col_ref[0] = inverse
    factor = {i: dot_nt(a_ref[left.index((i, j))], inverse) for i in range(j + 1, BLOCKS)}
    for i in factor:
        col_ref[i - j] = factor[i]
    for n, (i, k) in enumerate(later):
        rest_ref[n] = a_ref[left.index((i, k))] - dot_nt(factor[i], factor[k])


def solve_gram_kernel(core_ref, *refs):
    *cols, own_ref, other_ref, image_ref, out_ref, solved_ref = refs
    width = own_ref.shape[1]
    solved = []
    for j in range(BLOCKS):
        here = pl.ds(TILE * j, TILE)
        rest = jnp.concatenate([own_ref[here, :], other_ref[here, :]], axis=1)
        for i in range(j):
            rest = rest - dot_nn(cols[i][j - i], solved[i])
        solved.append(dot_nn(cols[j][0], rest))
        solved_ref[here, :] = solved[j]
        image_ref[here, :] = solved[j][:, :width]
    gram_half(core_ref[0], [solved_ref], out_ref)


def swap_core(x):
    return lax.ppermute(x, "core", [(0, 1), (1, 0)])


def shift(x, step, turned):
    side_x, side_y = lax.axis_size("x"), lax.axis_size("y")
    pairs = []
    for i in range(side_x):
        for j in range(side_y):
            for core in range(2):
                to = (i + step) % side_x, j
                if turned != bool(core):
                    to = i, (j + step) % side_y
                pairs.append(((i * side_y + j) * 2 + core, (to[0] * side_y + to[1]) * 2 + core))
    return lax.ppermute(x, ROWS, pairs)


def gather_line(x):
    return [shift(x, step, False) for step in (1, 2, 3)]


def gather_plane(line):
    return [line] + [shift(line, step, True) for step in (1, 2, 3)]


def gather_cores(lines, beside):
    first = swap_core(lines[0])
    rest, beside = lax.optimization_barrier((lines[1:], beside))
    return [lines[0], *rest, first, *map(swap_core, rest)], beside


def line_slot(column):
    core = column % 2
    along_x = (lax.axis_index("x") - column // 8) % 4
    along_y = (lax.axis_index("y") - column // 2 % 4) % 4
    inside = jnp.where(core == 0, along_y * 4 + along_x, along_x * 4 + along_y)
    return inside + jnp.where(core == lax.axis_index("core"), 0, 16)


def ring_sum(far, parts, work=(), state=()):
    size = lax.axis_size("z")

    def up(x):
        return lax.ppermute(x, "z", [(i, (i + 1) % size) for i in range(size)])

    def down(x):
        return lax.ppermute(x, "z", [((i + 1) % size, i) for i in range(size)])

    half = far.shape[1]
    right = jnp.pad(up(far[0]), ((0, half), (0, 0)))
    left = jnp.pad(down(far[1]), ((half, 0), (0, 0)))
    for step in range(1, FAR):
        right, left, state = lax.optimization_barrier(
            (parts[FAR - step] + right, parts[FAR + step] + left, state)
        )
        right, left = up(right), down(left)
        if work:
            state = work[step - 1](state)
            right, left, state = lax.optimization_barrier((right, left, state))
    return parts[0] + right + left, state


def plane_sum(part):
    plane = lax.axis_size(PLANE)
    part = part.reshape(plane, HALF * TILE // plane, TILE)
    return jnp.sum(lax.all_to_all(part, PLANE, 0, 0), axis=0)


def depth_sum(part):
    part = jnp.broadcast_to(part[None], (lax.axis_size("z"),) + part.shape)
    return jnp.sum(lax.all_to_all(part, "z", 0, 0), axis=0)


def plane_gather(part):
    part = jnp.broadcast_to(part[None], (lax.axis_size(PLANE),) + part.shape)
    part = lax.all_to_all(part, PLANE, 0, 0).reshape(HALF, TILE, TILE)
    return part, swap_core(part)


def local(basis, tile_counts, tile_rows, tile_cols, tile_live, marginals):
    width_k, terms_here = basis.shape
    capacity, tile_size, _ = tile_counts.shape
    row_count = lax.axis_size(ROWS)
    col_count = lax.axis_size("z")
    row_index = lax.axis_index(ROWS)
    col_index = lax.axis_index("z")
    core = lax.axis_index("core").astype(jnp.int32).reshape(1)
    group_size = row_count * terms_here
    block = basis.astype(jnp.bfloat16)
    line = jnp.stack([block] + gather_line(block))
    line, marginals, tile_rows, tile_cols, tile_live = lax.optimization_barrier(
        (line, marginals, tile_rows, tile_cols, tile_live)
    )
    lines = gather_plane(line)
    marg_float = marginals.astype(jnp.float32)
    grand_total = jnp.sum(marg_float)
    log_margins = jnp.log(marg_float)
    row_logs = lax.dynamic_index_in_dim(
        log_margins.reshape(col_count, row_count, terms_here), row_index, 1, keepdims=False
    )
    col_logs = lax.dynamic_slice_in_dim(log_margins, col_index * group_size, group_size).reshape(
        -1, tile_size
    )
    log_ratio = (
        jnp.log(jnp.maximum(tile_counts.astype(jnp.float32), 1.0))
        + jnp.log(grand_total)
        - jnp.take(row_logs, tile_rows, axis=0)[:, :, None]
        - jnp.take(col_logs, tile_cols, axis=0)[:, None, :]
    )
    position = jnp.arange(capacity, dtype=jnp.int32)
    keep_mask = (tile_counts > 0) & (position < tile_live[0])[:, None, None]
    ppmi = jnp.where(keep_mask, jnp.maximum(log_ratio, 0.0), 0.0).astype(jnp.bfloat16)
    lines, ppmi = gather_cores(lines, ppmi)
    distance = (tile_rows - col_index) % col_count

    slots = line_slot(tile_cols)

    def listed(farthest):
        chosen = ((distance == FAR) == farthest) & (position < tile_live[0])
        rank = jnp.sum((chosen[None, :] & (position[None, :] < position[:, None])).astype(jnp.int32), axis=1)
        placed = chosen[:, None] & (rank[:, None] == position[None, :])

        def pick(values):
            return jnp.sum(jnp.where(placed, values[:, None], 0), axis=0)

        count = jnp.sum(chosen.astype(jnp.int32))
        rows = jnp.where(position < count, pick(distance), 0 if farthest else FAR)
        return ((count + GROUP - 1) // GROUP).reshape(1), pick(position), rows, pick(slots)

    lists = {farthest: listed(farthest) for farthest in (True, False)}
    float_shape = functools.partial(jax.ShapeDtypeStruct, dtype=jnp.float32)
    half = width_k // 2
    shapes = {
        True: float_shape((2, half, terms_here)),
        False: float_shape((col_count, width_k, terms_here)),
    }

    def first_product(farthest):
        return call(
            functools.partial(multiply_kernel, farthest),
            shapes[farthest],
            [SMEM] * 4 + [VMEM] + [ANY] * len(lines),
            [
                pltpu.VMEM((row_count, width_k, terms_here), jnp.bfloat16),
                pltpu.SemaphoreType.DMA((len(lines),)),
            ],
            flops=2**30 if farthest else 2**32,
        )(*lists[farthest], ppmi, *lines)

    def second_product(farthest, lines):
        depth = 4 * GROUP
        return call(
            functools.partial(image_multiply_kernel, farthest),
            shapes[farthest],
            [SMEM] * 4 + [VMEM] + [ANY] * len(lines),
            [
                pltpu.VMEM((depth, width_k, terms_here), jnp.float32),
                pltpu.VMEM((GROUP, 2 * width_k, terms_here), jnp.bfloat16),
                pltpu.SemaphoreType.DMA((depth,)),
            ],
            flops=2**30 if farthest else 2**32,
        )(*lists[farthest], ppmi, *lines)

    square = pltpu.VMEM((TILE, TILE), jnp.float32)
    blocks = pltpu.VMEM((len(PAIRS), TILE, TILE), jnp.float32)

    def factor_step(j, *given):
        shape = [float_shape((BLOCKS - j, TILE, TILE))]
        if j + 1 < BLOCKS:
            shape.append(float_shape((len([pair for pair in PAIRS if pair[1] > j]), TILE, TILE)))
        return call(
            functools.partial(step_kernel, j),
            shape,
            [VMEM] if j else [SMEM, VMEM, VMEM],
            [square, square] if j else [square, square, blocks],
            flops=2**32,
        )(*given)

    def next_step(state):
        cols, rest = state
        col, *rest = factor_step(len(cols), *rest)
        return [*cols, col], rest

    solve = call(
        solve_kernel, float_shape((width_k, terms_here)), [SMEM] + [VMEM] * 3, [blocks, square, square]
    )
    gram_shape = float_shape((HALF, TILE, TILE))
    gram = call(gram_kernel, gram_shape, [SMEM, VMEM, VMEM])
    solve_gram = call(
        solve_gram_kernel,
        [float_shape((width_k, terms_here)), gram_shape],
        [SMEM] + [VMEM] * (BLOCKS + 2),
        [pltpu.VMEM((width_k, 2 * terms_here), jnp.float32)],
    )
    image, _ = ring_sum(first_product(True), first_product(False))
    near = gather_line(image)
    part = gram(core, image, swap_core(image))
    near, part = lax.optimization_barrier((near, part))
    near, part = lax.optimization_barrier((near, plane_sum(part)))
    line, part = lax.optimization_barrier((jnp.stack([image] + near), part))
    lines, part = lax.optimization_barrier((gather_plane(line), depth_sum(part)))
    lines += [swap_core(line) for line in lines]
    own, other = plane_gather(part)
    work = [next_step, next_step, lambda state: next_step(next_step(state))]
    state = ([], [core, own, other])
    product, (cols, _) = ring_sum(second_product(True, lines), second_product(False, lines), work, state)
    image, part = solve_gram(core, *cols, product, swap_core(product))
    return solve(core, *plane_gather(depth_sum(plane_sum(part))), image)


def solution(mesh):
    rows, cols = mesh.shape["rows"], mesh.shape["cols"]
    side = 4
    devices = mesh.devices.reshape(side, rows // (2 * side), 2, cols)
    inner = Mesh(devices, ("x", "y", "core", "z"))
    lists = (*ROWS, "z")
    terms = ("z", *ROWS)
    in_specs = (P(None, terms), P(lists, None, None), P(lists), P(lists), P(lists), P())
    return jax.shard_map(
        local, mesh=inner, in_specs=in_specs, out_specs=P(None, terms), check_vma=False
    )
```

```python
import functools

import jax
import jax.numpy as jnp
from jax import lax
from jax.experimental import pallas as pl
from jax.experimental.pallas import tpu as pltpu
from jax.sharding import Mesh, PartitionSpec as P

HIGHEST = lax.Precision.HIGHEST
TILE = 128
SUB = 8
BLOCKS = 4
PAIRS = [(i, j) for i in range(BLOCKS) for j in range(i + 1)]
PLACE = {pair: n for n, pair in enumerate(PAIRS)}
HALF = len(PAIRS) // 2
FAR = 4
PART = 64
GROUP = 4
ROWS = ("x", "y", "core")
PLANE = ("x", "y")
VMEM = pl.BlockSpec(memory_space=pltpu.VMEM)
ANY = pl.BlockSpec(memory_space=pl.ANY)
SMEM = pl.BlockSpec(memory_space=pltpu.SMEM)


def dot_nt(a, b, precision=HIGHEST):
    return lax.dot_general(
        a, b, (((1,), (1,)), ((), ())), precision=precision, preferred_element_type=jnp.float32
    )


def dot_nn(a, b):
    return jnp.dot(a, b, precision=HIGHEST, preferred_element_type=jnp.float32)


def call(kernel, out_shape, in_specs, scratch=(), mib=16, flops=0):
    return pl.pallas_call(
        kernel,
        out_shape=out_shape,
        in_specs=in_specs,
        out_specs=jax.tree.map(lambda shape: VMEM, out_shape),
        scratch_shapes=list(scratch),
        compiler_params=pltpu.CompilerParams(vmem_limit_bytes=mib * 1024 * 1024),
        cost_estimate=pl.CostEstimate(flops=flops, bytes_accessed=2**22, transcendentals=0),
    )


def add_products(farthest, out_ref, rows, products):
    half = out_ref.shape[1]
    for distance, product in zip(rows, products):
        if farthest:
            product = jnp.where(distance == FAR, product, 0.0)
            for n in range(2):
                out_ref[n] = out_ref[n] + product[n * half : (n + 1) * half]
        else:
            out_ref[distance] = out_ref[distance] + product


def multiply_kernel(farthest, count_ref, tiles_ref, rows_ref, cols_ref, ppmi_ref, *refs):
    *pieces, out_ref, basis_ref, sems = refs
    size = pieces[0].shape[0]
    copies = [
        pltpu.make_async_copy(piece, basis_ref.at[pl.ds(n * size, size)], sems.at[n])
        for n, piece in enumerate(pieces)
    ]
    for copy in copies:
        copy.start()
    out_ref[...] = jnp.zeros_like(out_ref)
    for copy in copies:
        copy.wait()

    def add_tiles(group, carry):
        members = [group * GROUP + n for n in range(GROUP)]
        products = [dot_nt(basis_ref[cols_ref[n]], ppmi_ref[tiles_ref[n]], None) for n in members]
        add_products(farthest, out_ref, [rows_ref[n] for n in members], products)
        return carry

    lax.fori_loop(0, count_ref[0], add_tiles, 0)


def image_multiply_kernel(farthest, count_ref, tiles_ref, rows_ref, cols_ref, ppmi_ref, *refs):
    *pieces, out_ref, columns_ref, parts_ref, sems = refs
    count = count_ref[0] * GROUP
    depth = columns_ref.shape[0]
    width = columns_ref.shape[1]
    size = pieces[0].shape[0]

    def copy(piece, entry, n):
        slot = lax.rem(n, depth)
        return pltpu.make_async_copy(piece.at[entry], columns_ref.at[slot], sems.at[slot])

    def fetch(n):
        place = cols_ref[n]
        for k, piece in enumerate(pieces):

            @pl.when(place // size == k)
            def _():
                copy(piece, place % size, n).start()

    for n in range(depth - GROUP):

        @pl.when(n < count)
        def _():
            fetch(n)

    out_ref[...] = jnp.zeros_like(out_ref)

    def add_tiles(group, carry):
        members = [group * GROUP + n for n in range(GROUP)]
        for n in members:

            @pl.when(n + depth - GROUP < count)
            def _():
                fetch(n + depth - GROUP)

        products = []
        for n in members:
            copy(pieces[0], 0, n).wait()
        for k, n in enumerate(members):
            column = columns_ref[lax.rem(n, depth)]
            high = column.astype(jnp.bfloat16)
            parts_ref[k, pl.ds(0, width), :] = high
            parts_ref[k, pl.ds(width, width), :] = (column - high.astype(jnp.float32)).astype(jnp.bfloat16)
            product = dot_nt(parts_ref[k], ppmi_ref[tiles_ref[n]], None)
            products.append(product[:width] + product[width:])
        add_products(farthest, out_ref, [rows_ref[n] for n in members], products)
        return carry

    lax.fori_loop(0, count_ref[0], add_tiles, 0)


def gram_half(core, parts, out_ref):
    for n in range(HALF):
        first, second = PAIRS[n], PAIRS[HALF + n]
        i = pl.multiple_of(jnp.where(core == 0, first[0], second[0]) * TILE, TILE)
        j = pl.multiple_of(jnp.where(core == 0, first[1], second[1]) * TILE, TILE)
        out_ref[n] = sum(dot_nt(ref[pl.ds(i, TILE), :], ref[pl.ds(j, TILE), :]) for ref in parts)


def gram_kernel(core_ref, own_ref, other_ref, out_ref):
    gram_half(core_ref[0], [own_ref, other_ref], out_ref)


def spread_row(x, m):
    return jnp.broadcast_to(x[m : m + 1, :], (SUB, TILE))


def spread_col(x, lane):
    return jnp.broadcast_to(x[:, lane : lane + 1], (SUB, TILE))


def eliminate(a, base, keep, write, c_ref):
    lane = lax.broadcasted_iota(jnp.int32, (SUB, TILE), 1)
    n = len(a)
    for p in range(n):
        first = base + SUB * p
        inside = (lane >= first) & (lane < first + SUB)
        cols = [[spread_col(a[i], first + k) for i in range(p, n)] for k in range(SUB)]
        place = PART * (p % 2)
        for k in range(SUB):
            c_ref[pl.ds(place + SUB * k, SUB), :] = cols[k][0]
        s = [[None] * SUB for _ in range(SUB)]
        for q in range(SUB):
            for k in range(q + 1):
                s[q][k] = jnp.broadcast_to(c_ref[pl.ds(place + SUB * k + q, 1), :], (SUB, TILE))
        t = [
            jnp.where(inside, jnp.where(lane == first + k, 1.0, 0.0), spread_row(a[p], k))
            for k in range(SUB)
        ]
        following = [cols[k][1] for k in range(SUB)] if p + 1 < n else None
        low = [[None] * SUB for _ in range(SUB)]
        inverse = [None] * SUB
        for k in range(SUB):
            inverse[k] = pl.reciprocal(s[k][k], approx=True)
            for q in range(k + 1, SUB):
                low[q][k] = s[q][k] * inverse[k]
            for q in range(k + 1, SUB):
                for j in range(k + 1, q + 1):
                    if q == k + 1:
                        s[q][j] = s[q][j] - (s[q][k] * s[j][k]) * inverse[k]
                    else:
                        s[q][j] = s[q][j] - low[q][k] * s[j][k]
            for q in range(k + 1, SUB):
                t[q] = t[q] - low[q][k] * t[k]
                if following is not None:
                    following[q] = following[q] - low[q][k] * following[k]
        shown = (lane < first + SUB) | (lane >= keep)
        for k in range(SUB):
            write(first + k, jnp.where(shown, t[k] * lax.rsqrt(s[k][k]), 0.0))
        if following is None:
            break
        t = [t[k] * inverse[k] for k in range(SUB)]
        x = jnp.where(inside, 0.0, a[p + 1])
        for k in range(SUB):
            x = x - following[k] * t[k]
        a[p + 1] = x
        z = [None] * SUB
        for k in reversed(range(SUB)):
            x = t[k]
            for q in range(k + 1, SUB):
                x = x - low[q][k] * z[q]
            z[k] = x
        for i in range(p + 2, n):
            x = jnp.where(inside, 0.0, a[i])
            for k in range(SUB):
                x = x - cols[k][i - p] * z[k]
            a[i] = x


def factor_inverse(read, w_ref, c_ref):
    a = [read(i) for i in range(TILE // SUB)]
    lane = lax.broadcasted_iota(jnp.int32, (PART, TILE), 1)

    def write(r, value):
        w_ref[pl.ds(r, 1), :] = value[0:1, :]

    step = PART // SUB
    eliminate(a[:step], 0, PART, write, c_ref)
    top = w_ref[pl.ds(0, PART), :]
    w_ref[pl.ds(0, PART), :] = jnp.where(lane < PART, top, 0.0)
    change = lax.dot_general(
        top, top, (((0,), (0,)), ((), ())), precision=HIGHEST, preferred_element_type=jnp.float32
    )
    a = [
        jnp.where(lane[:SUB] < PART, 0.0, a[i]) - change[SUB * i : SUB * (i + 1), :]
        for i in range(step, TILE // SUB)
    ]
    eliminate(a, PART, TILE, write, c_ref)


def factorize(core_ref, own_ref, other_ref, a_ref, w_ref, c_ref, step):
    core = core_ref[0]
    for n in range(HALF):
        a_ref[core * HALF + n] = own_ref[n]
        a_ref[(1 - core) * HALF + n] = other_ref[n]
    factor = {}
    for j in range(BLOCKS):
        here = PLACE[j, j]

        def read(i):
            return a_ref[here, pl.ds(SUB * i, SUB), :]

        factor_inverse(read, w_ref, c_ref)
        inverse = w_ref[...]
        for i in range(j + 1, BLOCKS):
            factor[i, j] = dot_nt(a_ref[PLACE[i, j]], inverse)
        for i in range(j + 1, BLOCKS):
            for k in range(j + 1, i + 1):
                n = PLACE[i, k]
                a_ref[n] = a_ref[n] - dot_nt(factor[i, j], factor[k, j])
        step(j, factor, inverse)


def solve_kernel(core_ref, own_ref, other_ref, image_ref, out_ref, a_ref, w_ref, c_ref):
    solved = []

    def step(j, factor, inverse):
        rest = image_ref[pl.ds(TILE * j, TILE), :]
        for i in range(j):
            rest = rest - dot_nn(factor[j, i], solved[i])
        solved.append(dot_nn(inverse, rest))
        out_ref[pl.ds(TILE * j, TILE), :] = solved[j]

    factorize(core_ref, own_ref, other_ref, a_ref, w_ref, c_ref, step)


def step_kernel(j, *refs):
    left = [pair for pair in PAIRS if pair[1] >= j]
    later = [pair for pair in PAIRS if pair[1] > j]
    rest_ref = None
    if j == 0:
        core_ref, own_ref, other_ref, col_ref, rest_ref, w_ref, c_ref, a_ref = refs
        core = core_ref[0]
        for n in range(HALF):
            a_ref[core * HALF + n] = own_ref[n]
            a_ref[(1 - core) * HALF + n] = other_ref[n]
    elif later:
        a_ref, col_ref, rest_ref, w_ref, c_ref = refs
    else:
        a_ref, col_ref, w_ref, c_ref = refs

    def read(i):
        return a_ref[left.index((j, j)), pl.ds(SUB * i, SUB), :]

    factor_inverse(read, w_ref, c_ref)
    inverse = w_ref[...]
    col_ref[0] = inverse
    factor = {i: dot_nt(a_ref[left.index((i, j))], inverse) for i in range(j + 1, BLOCKS)}
    for i in factor:
        col_ref[i - j] = factor[i]
    for n, (i, k) in enumerate(later):
        rest_ref[n] = a_ref[left.index((i, k))] - dot_nt(factor[i], factor[k])


def solve_gram_kernel(core_ref, *refs):
    *cols, own_ref, other_ref, image_ref, out_ref, solved_ref = refs
    width = own_ref.shape[1]
    solved = []
    for j in range(BLOCKS):
        here = pl.ds(TILE * j, TILE)
        rest = jnp.concatenate([own_ref[here, :], other_ref[here, :]], axis=1)
        for i in range(j):
            rest = rest - dot_nn(cols[i][j - i], solved[i])
        solved.append(dot_nn(cols[j][0], rest))
        solved_ref[here, :] = solved[j]
        image_ref[here, :] = solved[j][:, :width]
    gram_half(core_ref[0], [solved_ref], out_ref)


def swap_core(x):
    return lax.ppermute(x, "core", [(0, 1), (1, 0)])


def shift(x, step, turned):
    side_x, side_y = lax.axis_size("x"), lax.axis_size("y")
    pairs = []
    for i in range(side_x):
        for j in range(side_y):
            for core in range(2):
                to = (i + step) % side_x, j
                if turned != bool(core):
                    to = i, (j + step) % side_y
                pairs.append(((i * side_y + j) * 2 + core, (to[0] * side_y + to[1]) * 2 + core))
    return lax.ppermute(x, ROWS, pairs)


def gather_line(x):
    return [shift(x, step, False) for step in (1, 2, 3)]


def gather_plane(line):
    return [line] + [shift(line, step, True) for step in (1, 2, 3)]


def gather_cores(lines, beside):
    first = swap_core(lines[0])
    rest, beside = lax.optimization_barrier((lines[1:], beside))
    return [lines[0], *rest, first, *map(swap_core, rest)], beside


def line_slot(column):
    core = column % 2
    along_x = (lax.axis_index("x") - column // 8) % 4
    along_y = (lax.axis_index("y") - column // 2 % 4) % 4
    inside = jnp.where(core == 0, along_y * 4 + along_x, along_x * 4 + along_y)
    return inside + jnp.where(core == lax.axis_index("core"), 0, 16)


def ring_sum(far, parts, work=(), state=()):
    size = lax.axis_size("z")

    def up(x):
        return lax.ppermute(x, "z", [(i, (i + 1) % size) for i in range(size)])

    def down(x):
        return lax.ppermute(x, "z", [((i + 1) % size, i) for i in range(size)])

    half = far.shape[1]
    right = jnp.pad(up(far[0]), ((0, half), (0, 0)))
    left = jnp.pad(down(far[1]), ((half, 0), (0, 0)))
    for step in range(1, FAR):
        right, left, state = lax.optimization_barrier(
            (parts[FAR - step] + right, parts[FAR + step] + left, state)
        )
        right, left = up(right), down(left)
        if work:
            state = work[step - 1](state)
            right, left, state = lax.optimization_barrier((right, left, state))
    return parts[0] + right + left, state


def plane_sum(part):
    plane = lax.axis_size(PLANE)
    part = part.reshape(plane, HALF * TILE // plane, TILE)
    return jnp.sum(lax.all_to_all(part, PLANE, 0, 0), axis=0)


def depth_sum(part):
    part = jnp.broadcast_to(part[None], (lax.axis_size("z"),) + part.shape)
    return jnp.sum(lax.all_to_all(part, "z", 0, 0), axis=0)


def plane_gather(part):
    part = jnp.broadcast_to(part[None], (lax.axis_size(PLANE),) + part.shape)
    part = lax.all_to_all(part, PLANE, 0, 0).reshape(HALF, TILE, TILE)
    return part, swap_core(part)


def local(basis, tile_counts, tile_rows, tile_cols, tile_live, marginals):
    width_k, terms_here = basis.shape
    capacity, tile_size, _ = tile_counts.shape
    row_count = lax.axis_size(ROWS)
    col_count = lax.axis_size("z")
    row_index = lax.axis_index(ROWS)
    col_index = lax.axis_index("z")
    core = lax.axis_index("core").astype(jnp.int32).reshape(1)
    group_size = row_count * terms_here
    block = basis.astype(jnp.bfloat16)
    line = jnp.stack([block] + gather_line(block))
    line, marginals, tile_rows, tile_cols, tile_live = lax.optimization_barrier(
        (line, marginals, tile_rows, tile_cols, tile_live)
    )
    lines = gather_plane(line)
    marg_float = marginals.astype(jnp.float32)
    grand_total = jnp.sum(marg_float)
    log_margins = jnp.log(marg_float)
    row_logs = lax.dynamic_index_in_dim(
        log_margins.reshape(col_count, row_count, terms_here), row_index, 1, keepdims=False
    )
    col_logs = lax.dynamic_slice_in_dim(log_margins, col_index * group_size, group_size).reshape(
        -1, tile_size
    )
    log_ratio = (
        jnp.log(jnp.maximum(tile_counts.astype(jnp.float32), 1.0))
        + jnp.log(grand_total)
        - jnp.take(row_logs, tile_rows, axis=0)[:, :, None]
        - jnp.take(col_logs, tile_cols, axis=0)[:, None, :]
    )
    position = jnp.arange(capacity, dtype=jnp.int32)
    keep_mask = (tile_counts > 0) & (position < tile_live[0])[:, None, None]
    ppmi = jnp.where(keep_mask, jnp.maximum(log_ratio, 0.0), 0.0).astype(jnp.bfloat16)
    lines, ppmi = gather_cores(lines, ppmi)
    distance = (tile_rows - col_index) % col_count

    slots = line_slot(tile_cols)

    def listed(farthest):
        chosen = ((distance == FAR) == farthest) & (position < tile_live[0])
        rank = jnp.sum((chosen[None, :] & (position[None, :] < position[:, None])).astype(jnp.int32), axis=1)
        placed = chosen[:, None] & (rank[:, None] == position[None, :])

        def pick(values):
            return jnp.sum(jnp.where(placed, values[:, None], 0), axis=0)

        count = jnp.sum(chosen.astype(jnp.int32))
        rows = jnp.where(position < count, pick(distance), 0 if farthest else FAR)
        return ((count + GROUP - 1) // GROUP).reshape(1), pick(position), rows, pick(slots)

    lists = {farthest: listed(farthest) for farthest in (True, False)}
    float_shape = functools.partial(jax.ShapeDtypeStruct, dtype=jnp.float32)
    half = width_k // 2
    shapes = {
        True: float_shape((2, half, terms_here)),
        False: float_shape((col_count, width_k, terms_here)),
    }

    def first_product(farthest):
        return call(
            functools.partial(multiply_kernel, farthest),
            shapes[farthest],
            [SMEM] * 4 + [VMEM] + [ANY] * len(lines),
            [
                pltpu.VMEM((row_count, width_k, terms_here), jnp.bfloat16),
                pltpu.SemaphoreType.DMA((len(lines),)),
            ],
            flops=2**30 if farthest else 2**32,
        )(*lists[farthest], ppmi, *lines)

    def second_product(farthest, lines):
        depth = 2 * GROUP
        return call(
            functools.partial(image_multiply_kernel, farthest),
            shapes[farthest],
            [SMEM] * 4 + [VMEM] + [ANY] * len(lines),
            [
                pltpu.VMEM((depth, width_k, terms_here), jnp.float32),
                pltpu.VMEM((GROUP, 2 * width_k, terms_here), jnp.bfloat16),
                pltpu.SemaphoreType.DMA((depth,)),
            ],
            flops=2**30 if farthest else 2**32,
        )(*lists[farthest], ppmi, *lines)

    square = pltpu.VMEM((TILE, TILE), jnp.float32)
    blocks = pltpu.VMEM((len(PAIRS), TILE, TILE), jnp.float32)

    def factor_step(j, *given):
        shape = [float_shape((BLOCKS - j, TILE, TILE))]
        if j + 1 < BLOCKS:
            shape.append(float_shape((len([pair for pair in PAIRS if pair[1] > j]), TILE, TILE)))
        return call(
            functools.partial(step_kernel, j),
            shape,
            [VMEM] if j else [SMEM, VMEM, VMEM],
            [square, square] if j else [square, square, blocks],
            flops=2**32,
        )(*given)

    def next_step(state):
        cols, rest = state
        col, *rest = factor_step(len(cols), *rest)
        return [*cols, col], rest

    solve = call(
        solve_kernel, float_shape((width_k, terms_here)), [SMEM] + [VMEM] * 3, [blocks, square, square]
    )
    gram_shape = float_shape((HALF, TILE, TILE))
    gram = call(gram_kernel, gram_shape, [SMEM, VMEM, VMEM])
    solve_gram = call(
        solve_gram_kernel,
        [float_shape((width_k, terms_here)), gram_shape],
        [SMEM] + [VMEM] * (BLOCKS + 2),
        [pltpu.VMEM((width_k, 2 * terms_here), jnp.float32)],
    )
    image, _ = ring_sum(first_product(True), first_product(False))
    near = gather_line(image)
    part = gram(core, image, swap_core(image))
    near, part = lax.optimization_barrier((near, part))
    near, part = lax.optimization_barrier((near, plane_sum(part)))
    line, part = lax.optimization_barrier((jnp.stack([image] + near), part))
    lines, part = lax.optimization_barrier((gather_plane(line), depth_sum(part)))
    lines += [swap_core(line) for line in lines]
    own, other = plane_gather(part)
    work = [next_step, next_step, lambda state: next_step(next_step(state))]
    state = ([], [core, own, other])
    product, (cols, _) = ring_sum(second_product(True, lines), second_product(False, lines), work, state)
    image, part = solve_gram(core, *cols, product, swap_core(product))
    return solve(core, *plane_gather(depth_sum(plane_sum(part))), image)


def solution(mesh):
    rows, cols = mesh.shape["rows"], mesh.shape["cols"]
    side = 4
    devices = mesh.devices.reshape(side, rows // (2 * side), 2, cols)
    inner = Mesh(devices, ("x", "y", "core", "z"))
    lists = (*ROWS, "z")
    terms = ("z", *ROWS)
    in_specs = (P(None, terms), P(lists, None, None), P(lists), P(lists), P(lists), P())
    return jax.shard_map(
        local, mesh=inner, in_specs=in_specs, out_specs=P(None, terms), check_vma=False
    )
```
